128 devices in a mesh: ctx: 32 (over z_hi, y, x), head: 4 (over z_lo, core).
Axes of the slice: x: 4, y: 4, z: 4 (z_hi: 2, z_lo: 2; z = z_hi * 2 + z_lo), core: 2. Of those that a mesh axis runs over, the one named last changes fastest.
Arguments:
- query: bfloat16 [24576, 2048], P('ctx', 'head'), may hold values from -0.625 to 0.625
- keys: bfloat16 [24576, 2048], P('ctx', 'head'), may hold values from -6 to 6
- values: bfloat16 [24576, 4096], P('ctx', 'head'), may hold values from -0.3125 to 0.3125
- out_grad: bfloat16 [24576, 2048], P('ctx', 'head'), may hold values from -6 to 6
- out_weight: bfloat16 [4096, 2048], P('head'), may hold values from -0.125 to 0.125
- log_decay: float32 [16, 24576], P('head', 'ctx'), may hold values from -1 to 0
- block_order: int32 [64], replicated, may hold values from 0 to 63, each once
Outputs:
- query_grad: bfloat16 [24576, 2048], P('ctx', 'head')
- key_grad: bfloat16 [24576, 2048], P('ctx', 'head')
- value_grad: bfloat16 [24576, 4096], P('ctx', 'head')
The draws below stay inside these ranges and needn't reach their ends.
Inputs may be any that keep to these rules, and one draw needn't show every extreme that they name: `block_order`: each of the 64 sequence blocks is named once.
All inputs are finite; a program needn't handle non-finite values.
Results may differ from the reference program's by a relative error of at most 0.0058.
Values may be sent and summed in bfloat16 or wider, within the bound.
A program may use at most 128 MiB of HBM per device.

```python
import math
import jax
import jax.numpy as jnp
from jax import lax

D = 2048
HEAD_TOTAL = 16
DK = 128
DV = 256
TOK_DEV = 768
REACH = 2
BLK = 384
BLOCKS = 64
GROUPS = 32
TOKEN_TOTAL = 24576


def draw_log_decay(key, part):
    key = jax.random.fold_in(key, 11)
    rates_random_key, noise_random_key, spike_random_key, level_random_key = jax.random.split(key, 4)
    lower_log = math.log(0.2 / TOKEN_TOTAL)
    upper_log = math.log(1.0 / 32.0)
    per_head_rates = jnp.exp(jax.random.uniform(rates_random_key, (HEAD_TOTAL, 1), jnp.float32, lower_log, upper_log))
    random_noise = jnp.exp(jax.random.uniform(noise_random_key, (HEAD_TOTAL, TOKEN_TOTAL), jnp.float32, math.log(0.5), math.log(2.0)))
    decay_spikes = jax.random.randint(spike_random_key, (HEAD_TOTAL, TOKEN_TOTAL), 0, max(TOKEN_TOTAL // 3, 2)) == 0
    decay_levels = jax.random.uniform(level_random_key, (HEAD_TOTAL, TOKEN_TOTAL), jnp.float32, 0.22, 0.69)
    return -(per_head_rates * random_noise) - jnp.where(decay_spikes, decay_levels, 0.0)


def levels(key, shape, shards, low, top_value):
    def one(position, blocks):
        heights = jax.random.uniform(jax.random.fold_in(jax.random.fold_in(key, 6), position), (blocks,), jnp.float32, low / len(shards), top_value / len(shards))
        return jnp.repeat(jnp.exp(heights), shape[position] // blocks).reshape((-1,) + (1,) * (len(shape) - position - 1))

    gain = one(*shards[0])
    for cut in shards[1:]:
        gain = gain * one(*cut)
    return gain


def noise(own_key, extent, width, bound, shards=(), held_as=jnp.bfloat16):
    entries = width * jax.random.normal(own_key, extent, jnp.float32)
    if shards:
        entries = entries * levels(own_key, extent, shards, -0.22, 0.18)
    return jnp.clip(entries, -bound, bound).astype(held_as)


def setup_inputs(seed: int = 0) -> dict:
    key_list = jax.random.split(jax.random.key(seed), 8)
    query = noise(key_list[0], (TOKEN_TOTAL, HEAD_TOTAL * DK), 0.1, 0.625, ((0, 32), (1, 4)))
    keys = noise(key_list[1], (TOKEN_TOTAL, HEAD_TOTAL * DK), 1.0, 6.0, ((0, 32), (1, 4)))
    values = noise(key_list[2], (TOKEN_TOTAL, HEAD_TOTAL * DV), 0.05, 0.3125, ((0, 32), (1, 4)))
    out_grad = noise(key_list[3], (TOKEN_TOTAL, D), 1.0, 6.0, ((0, 32), (1, 4)))
    out_weight = noise(key_list[4], (HEAD_TOTAL * DV, D), D ** -0.5, 0.125, ((0, 4),))
    log_decay = draw_log_decay(jax.random.fold_in(key_list[7], 71), 0)
    block_order = jax.random.permutation(key_list[6], BLOCKS).astype(jnp.int32)
    return {"query": query, "keys": keys, "values": values, "out_grad": out_grad, "out_weight": out_weight, "log_decay": log_decay, "block_order": block_order}


def reference(query, keys, values, out_grad, out_weight, log_decay, block_order):
    array_rows = jnp.arange(TOKEN_TOTAL, dtype=jnp.int32)
    positions = (block_order[array_rows // BLK] * BLK + array_rows % BLK).astype(jnp.int32)
    in_order = jnp.argsort(positions).astype(jnp.int32)
    d_out = jnp.dot(out_grad, out_weight.T, preferred_element_type=jnp.float32).astype(jnp.bfloat16)
    cumulative = jnp.cumsum(log_decay[:, in_order], axis=1)[:, positions]
    score_scale = DK ** -0.5
    query_dev = query.reshape(GROUPS, TOK_DEV, HEAD_TOTAL, DK)
    keys_dev = keys.reshape(GROUPS, TOK_DEV, HEAD_TOTAL, DK)
    values_dev = values.reshape(GROUPS, TOK_DEV, HEAD_TOTAL, DV)
    grads_dev = d_out.reshape(GROUPS, TOK_DEV, HEAD_TOTAL, DV)
    pos_dev = positions.reshape(GROUPS, TOK_DEV)
    cum_dev = cumulative.reshape(HEAD_TOTAL, GROUPS, TOK_DEV).transpose(1, 0, 2)
    reach_steps = jnp.arange(REACH + 1, dtype=jnp.int32)

    def rows_of(array, groups):
        picked = array[groups]
        return picked.reshape((-1,) + picked.shape[2:])

    def cum_rows(groups):
        return cum_dev[groups].transpose(1, 0, 2).reshape(HEAD_TOTAL, -1)

    def decay_of(late_pos, late_cum, early_pos, early_cum):
        causal = late_pos[:, None] >= early_pos[None, :]
        log_gap = late_cum[:, :, None] - early_cum[:, None, :]
        return jnp.where(causal[None], jnp.exp(jnp.minimum(log_gap, 0.0)), 0.0)

    def weights_of(late_grads, early_values, decay):
        grad_scores = jnp.einsum("thv,shv->hts", late_grads.astype(jnp.float32), early_values.astype(jnp.float32))
        return ((grad_scores * decay) * score_scale).astype(jnp.bfloat16)

    def probs_of(late_query, early_keys, decay):
        scores = jnp.einsum("thd,shd->hts", late_query.astype(jnp.float32), early_keys.astype(jnp.float32))
        return ((scores * score_scale) * decay).astype(jnp.bfloat16)

    def query_side(group):
        sources = ((group - reach_steps) % GROUPS).astype(jnp.int32)
        early_keys = rows_of(keys_dev, sources)
        decay = decay_of(pos_dev[group], cum_dev[group], pos_dev[sources].reshape(-1), cum_rows(sources))
        grad_weights = weights_of(grads_dev[group], rows_of(values_dev, sources), decay)
        part = jnp.einsum("hts,shd->thd", grad_weights.astype(jnp.float32), early_keys.astype(jnp.float32))
        return part.astype(jnp.bfloat16)

    def key_side(group):
        sinks = ((group + reach_steps) % GROUPS).astype(jnp.int32)
        late_query = rows_of(query_dev, sinks)
        late_grads = rows_of(grads_dev, sinks)
        decay = decay_of(pos_dev[sinks].reshape(-1), cum_rows(sinks), pos_dev[group], cum_dev[group])
        probs = probs_of(late_query, keys_dev[group], decay)
        grad_weights = weights_of(late_grads, values_dev[group], decay)
        key_part = jnp.einsum("hts,thd->shd", grad_weights.astype(jnp.float32), late_query.astype(jnp.float32))
        value_part = jnp.einsum("hts,thv->shv", probs.astype(jnp.float32), late_grads.astype(jnp.float32))
        return key_part.astype(jnp.bfloat16), value_part.astype(jnp.bfloat16)

    group_ids = jnp.arange(GROUPS, dtype=jnp.int32)
    query_grad = lax.map(query_side, group_ids)
    key_grad, value_grad = lax.map(key_side, group_ids)
    return (query_grad.reshape(TOKEN_TOTAL, HEAD_TOTAL * DK), key_grad.reshape(TOKEN_TOTAL, HEAD_TOTAL * DK),
            value_grad.reshape(TOKEN_TOTAL, HEAD_TOTAL * DV))
```

```python
import jax
import jax.numpy as jnp
from jax import lax
from jax.experimental import pallas as pl
from jax.experimental.pallas import tpu as pltpu
from jax.sharding import PartitionSpec as P

MESH = pl.DeviceIdType.MESH
F32 = jnp.float32
BF16 = jnp.bfloat16
HEADS = 4
DK = 128
DV = 256
BLK = 384
ROWS = 768
COLS = 512
TILE = 128
GROUPS = 32
SCALE = DK ** -0.5

NT = (((1,), (1,)), ((), ()))
NN = (((1,), (0,)), ((), ()))
TN = (((0,), (0,)), ((), ()))


def dot(a, b, dims):
    return lax.dot_general(a, b, dims, preferred_element_type=F32)


def exact_dot(a, b, dims):
    return lax.dot_general(
        a, b, dims, preferred_element_type=F32, precision=lax.Precision.HIGHEST
    )


def kernel(
    q_hbm, k_hbm, v_hbm, og_hbm, w_hbm, ld_hbm, bo_hbm,
    dq_hbm, dk_hbm, dv_hbm,
    q, k, v, og, w, ld, bo,
    lrow, lcol, qdec, kdec, qpt, dec, probs,
    part, d_out,
    n_own, n_one, n_two, m_own, m_one, m_two,
    totals, weights,
    dq_sum, dk_sum, dv_sum, dq_out, dk_out, dv_out,
    loc_sem, og_ss, og_rs, n_ss, n_rs, m_ss, m_rs, t_ss, t_rs, out_sem,
):
    c = lax.axis_index("ctx")
    p = lax.axis_index("head")
    x = lax.rem(c, 4)
    y = lax.rem(c // 4, 4)
    zh = c // 16
    core_mate = p + 1 - 2 * lax.rem(p, 2)
    z_mate = lax.rem(p + 2, 4)
    diag_mate = lax.rem(core_mate + 2, 4)
    later = lax.rem(c + 1, GROUPS)
    earlier = lax.rem(c + GROUPS - 1, GROUPS)
    x_peers = [c - x + lax.rem(x + a, 4) for a in (1, 2, 3)]
    y_peers = [c - 4 * y + 4 * lax.rem(y + a, 4) for a in (1, 2, 3)]
    zh_peer = lax.rem(c + 16, GROUPS)

    local = [
        pltpu.make_async_copy(src, dst, loc_sem.at[i])
        for i, (src, dst) in enumerate(
            ((ld_hbm, ld), (bo_hbm, bo), (k_hbm, k), (v_hbm, v), (q_hbm, q),
             (og_hbm, og.at[0]), (w_hbm, w))
        )
    ]
    for copy in local:
        copy.start()
    ld_in, bo_in, k_in, v_in, q_in, og_in, w_in = local

    barrier = pltpu.get_barrier_semaphore()
    partners = [(c, core_mate), (c, z_mate), (later, p), (earlier, p), (zh_peer, p)]
    partners += [(peer, p) for peer in x_peers + y_peers]
    for partner in partners:
        pl.semaphore_signal(barrier, inc=1, device_id=partner, device_id_type=MESH)
    pl.semaphore_wait(barrier, len(partners))

    def send(src, dst, ss, rs, to):
        return pltpu.make_async_remote_copy(
            src_ref=src, dst_ref=dst, send_sem=ss, recv_sem=rs, device_id=to, device_id_type=MESH
        )

    def rows_of(b):
        return pl.ds(b * BLK, BLK)

    z_copy = [
        send(og_hbm.at[rows_of(b)], og.at[2, rows_of(b)], og_ss.at[b], og_rs.at[b], (c, z_mate))
        for b in (0, 1)
    ]
    core_copy = [
        send(og_hbm.at[rows_of(b)], og.at[1, rows_of(b)], og_ss.at[2 + b], og_rs.at[2 + b],
             (c, core_mate))
        for b in (0, 1)
    ]
    diag_copy = [
        send(og.at[2, rows_of(b)], og.at[3, rows_of(b)], og_ss.at[4 + b], og_rs.at[4 + b],
             (c, core_mate))
        for b in (0, 1)
    ]
    n_copy = [send(n_own.at[b], n_one.at[b], n_ss.at[b], n_rs.at[b], (later, p)) for b in (0, 1)]
    n_pass = [
        send(n_one.at[b], n_two.at[b], n_ss.at[2 + b], n_rs.at[2 + b], (later, p)) for b in (0, 1)
    ]
    m_copy = [send(m_own.at[b], m_one.at[b], m_ss.at[b], m_rs.at[b], (earlier, p)) for b in (0, 1)]
    m_pass = [
        send(m_one.at[b], m_two.at[b], m_ss.at[2 + b], m_rs.at[2 + b], (earlier, p)) for b in (0, 1)
    ]
    tx_copy = [
        send(totals.at[pl.ds(c, 1)], totals.at[pl.ds(c, 1)], t_ss.at[a], t_rs.at[a], (x_peers[a], p))
        for a in range(3)
    ]
    ty_copy = [
        send(totals.at[pl.ds(c - x, 4)], totals.at[pl.ds(c - x, 4)], t_ss.at[3 + a], t_rs.at[3 + a],
             (y_peers[a], p))
        for a in range(3)
    ]
    tz_copy = send(
        totals.at[pl.ds(zh * 16, 16)], totals.at[pl.ds(zh * 16, 16)], t_ss.at[6], t_rs.at[6],
        (zh_peer, p),
    )

    for copy in z_copy + core_copy:
        copy.start()

    ld_in.wait()
    logs = jnp.concatenate([ld[:, :BLK], ld[:, BLK:]], axis=0)
    up_to = (
        lax.broadcasted_iota(jnp.int32, (BLK, BLK), 0)
        <= lax.broadcasted_iota(jnp.int32, (BLK, BLK), 1)
    ).astype(F32)
    lrow[...] = exact_dot(logs, up_to, NN).reshape(8, 1, BLK)
    total = exact_dot(logs, jnp.ones((BLK, TILE), F32), NN)
    totals[pl.ds(c, 1)] = total.reshape(1, 8, TILE)
    for copy in tx_copy:
        copy.start()
    columns = exact_dot(up_to, logs, (((0,), (1,)), ((), ())))
    for j in range(8):
        column = jnp.broadcast_to(columns[:, j : j + 1], (BLK, TILE))
        lcol[j] = column
        qdec[j] = jnp.exp(column)
        kdec[j] = jnp.exp(total[j : j + 1, :] - column)

    def key_cols(h):
        return pl.ds(pl.multiple_of(h * DK, DK), DK)

    def value_cols(h):
        return pl.ds(pl.multiple_of(h * DV, DV), DV)

    k_in.wait()
    v_in.wait()
    for b in (0, 1):
        for h in range(HEADS):
            scaled = (k[rows_of(b), key_cols(h)].astype(F32) * kdec[b * 4 + h]).astype(BF16)
            n_own[b, h] = dot(scaled, v[rows_of(b), value_cols(h)], TN).astype(BF16)
        n_copy[b].start()

    for copy in tx_copy:
        copy.wait_recv()
    for copy in ty_copy:
        copy.start()

    q_in.wait()

    def early_part(b, h):
        j = b * 4 + h
        scaled = (q[rows_of(b), key_cols(h)].astype(F32) * qdec[j]).astype(BF16)
        qpt[j] = jnp.transpose(scaled)
        for i in range(3):
            first = i * TILE
            width = BLK - first
            gap = lrow[j][:, first:] - jnp.concatenate(
                [lcol[j, pl.ds(first, TILE)]] * (width // TILE), axis=1
            )
            on = lax.broadcasted_iota(jnp.int32, (TILE, width), 1) >= lax.broadcasted_iota(
                jnp.int32, (TILE, width), 0
            )
            decay = jnp.where(on, jnp.exp(jnp.minimum(gap, 0.0)), 0.0) * SCALE
            dec[j, pl.ds(first, TILE), pl.ds(first, width)] = decay
            scores = dot(
                k[pl.ds(b * BLK + first, TILE), key_cols(h)],
                q[pl.ds(b * BLK + first, width), key_cols(h)],
                NT,
            )
            probs[j, pl.ds(first, TILE), pl.ds(first, width)] = (scores * decay).astype(BF16)

    for b in (0, 1):
        lax.fori_loop(0, HEADS, lambda h, _, b=b: (early_part(b, h), 0)[1], 0)

    for copy in ty_copy:
        copy.wait_recv()
    tz_copy.start()

    def product(slot, owner, b):
        return dot(
            og[slot, rows_of(b)], w[:, pl.ds(pl.multiple_of(owner * COLS, COLS), COLS)], NT
        )

    og_in.wait()
    w_in.wait()
    for b in (0, 1):
        core_copy[b].wait_recv()
        part[rows_of(b)] = product(0, p, b) + product(1, core_mate, b)

    def late_part(b, h):
        j = b * 4 + h
        for i in range(3):
            first = i * TILE
            width = BLK - first
            s_rows = pl.ds(b * BLK + first, TILE)
            t_rows = pl.ds(b * BLK + first, width)
            grads = d_out[t_rows, value_cols(h)]
            scores = dot(v[s_rows, value_cols(h)], grads, NT)
            grad_weights = (scores * dec[j, pl.ds(first, TILE), pl.ds(first, width)]).astype(BF16)
            dv_sum[s_rows, value_cols(h)] = dot(
                probs[j, pl.ds(first, TILE), pl.ds(first, width)], grads, NN
            )
            dk_sum[s_rows, key_cols(h)] = dot(grad_weights, q[t_rows, key_cols(h)], NN)
            to_query = dot(grad_weights, k[s_rows, key_cols(h)], TN)
            if i == 0:
                dq_sum[t_rows, key_cols(h)] = to_query
            else:
                dq_sum[t_rows, key_cols(h)] += to_query

    def gather_and_send(b):
        z_copy[b].wait_recv()
        diag_copy[b].start()
        part[rows_of(b)] += product(2, z_mate, b)
        diag_copy[b].wait_recv()
        d_out[rows_of(b)] = (part[rows_of(b)] + product(3, diag_mate, b)).astype(BF16)
        for h in range(HEADS):
            m_own[b, h] = dot(qpt[b * 4 + h], d_out[rows_of(b), value_cols(h)], NN).astype(BF16)
        m_copy[b].start()

    gather_and_send(0)
    n_copy[0].wait_recv()
    n_pass[0].start()
    lax.fori_loop(0, HEADS, lambda h, _: (late_part(0, h), 0)[1], 0)
    n_copy[1].wait_recv()
    n_pass[1].start()

    tz_copy.wait_recv()
    bo_in.wait()

    def place(group, b):
        return bo[2 * group + b]

    own = [place(c, b) for b in (0, 1)]
    late = [place(lax.rem(c + d, GROUPS), b) for d in (1, 2) for b in (0, 1)]
    early = [place(lax.rem(c + GROUPS - d, GROUPS), b) for d in (1, 2) for b in (0, 1)]
    pairs = [(o, own[b]) for b in (0, 1) for o in [own[1 - b]] + late]
    pairs += [(own[b], o) for b in (0, 1) for o in early]
    first_rows = lax.broadcasted_iota(jnp.int32, (8, TILE), 0) < 4

    def add_group(g, sums):
        at = jnp.where(first_rows, bo[2 * g], bo[2 * g + 1])
        tile = totals[g]
        return tuple(
            s + jnp.where((at > lo) & (at < hi), tile, 0.0) for s, (hi, lo) in zip(sums, pairs)
        )

    sums = lax.fori_loop(
        0, GROUPS, add_group, tuple(jnp.zeros((8, TILE), F32) for _ in pairs)
    )
    for n, (hi, lo) in enumerate(pairs):
        gap = sums[n][:4] + sums[n][4:]
        seen = jnp.full((4, TILE), hi, jnp.int32) > lo
        factor = jnp.where(seen, jnp.exp(gap), 0.0) * SCALE
        weights[n, :4] = jnp.concatenate([factor, factor], axis=1)

    def weighted(n, state, h):
        return weights[n, h : h + 1] * state.astype(F32)

    gather_and_send(1)
    lax.fori_loop(0, HEADS, lambda h, _: (late_part(1, h), 0)[1], 0)

    m_copy[0].wait_recv()
    m_pass[0].start()

    for copy in n_pass:
        copy.wait_recv()
    for b in (0, 1):
        for h in range(HEADS):
            state = weighted(5 * (1 - b), n_own[1 - b, h], h)
            for i, source in enumerate((n_one, n_two)):
                for other in (0, 1):
                    state = state + weighted(10 + 4 * b + 2 * i + other, source[other, h], h)
            rest = dot(d_out[rows_of(b), value_cols(h)], state.astype(BF16), NT)
            dq_out[rows_of(b), key_cols(h)] = (
                dq_sum[rows_of(b), key_cols(h)] + rest * qdec[b * 4 + h]
            ).astype(BF16)
    dq_done = pltpu.make_async_copy(dq_out, dq_hbm, out_sem.at[0])
    dq_done.start()

    m_copy[1].wait_recv()
    m_pass[1].start()
    for copy in m_pass:
        copy.wait_recv()
    for b in (0, 1):
        for h in range(HEADS):
            state = weighted(5 * b, m_own[1 - b, h], h)
            for i, source in enumerate((m_one, m_two)):
                for other in (0, 1):
                    state = state + weighted(5 * b + 1 + 2 * i + other, source[other, h], h)
            state = state.astype(BF16)
            decay = kdec[b * 4 + h]
            to_value = dot(k[rows_of(b), key_cols(h)], state, NN)
            to_key = dot(v[rows_of(b), value_cols(h)], state, NT)
            dv_out[rows_of(b), value_cols(h)] = (
                dv_sum[rows_of(b), value_cols(h)]
                + to_value * jnp.concatenate([decay, decay], axis=1)
            ).astype(BF16)
            dk_out[rows_of(b), key_cols(h)] = (
                dk_sum[rows_of(b), key_cols(h)] + to_key * decay
            ).astype(BF16)
    dk_done = pltpu.make_async_copy(dk_out, dk_hbm, out_sem.at[1])
    dv_done = pltpu.make_async_copy(dv_out, dv_hbm, out_sem.at[2])
    dk_done.start()
    dv_done.start()
    for copy in z_copy + core_copy + diag_copy + n_copy + n_pass + m_copy + m_pass:
        copy.wait_send()
    for copy in tx_copy + ty_copy + [tz_copy]:
        copy.wait_send()
    for copy in (dq_done, dk_done, dv_done):
        copy.wait()


def on_device(query, keys, values, out_grad, out_weight, log_decay, block_order):
    anywhere = pl.BlockSpec(memory_space=pl.ANY)
    vmem = pltpu.VMEM
    states = (2, HEADS, DK, DV)
    dma = pltpu.SemaphoreType.DMA
    return pl.pallas_call(
        kernel,
        name="retention_backward",
        out_shape=(
            jax.ShapeDtypeStruct((ROWS, HEADS * DK), BF16),
            jax.ShapeDtypeStruct((ROWS, HEADS * DK), BF16),
            jax.ShapeDtypeStruct((ROWS, HEADS * DV), BF16),
        ),
        in_specs=[anywhere] * 7,
        out_specs=(anywhere,) * 3,
        scratch_shapes=[
            vmem((ROWS, HEADS * DK), BF16),
            vmem((ROWS, HEADS * DK), BF16),
            vmem((ROWS, HEADS * DV), BF16),
            vmem((4, ROWS, COLS), BF16),
            vmem((HEADS * DV, 4 * COLS), BF16),
            vmem((HEADS, ROWS), F32),
            pltpu.SMEM((2 * GROUPS,), jnp.int32),
            vmem((8, 1, BLK), F32),
            vmem((8, BLK, TILE), F32),
            vmem((8, BLK, TILE), F32),
            vmem((8, BLK, TILE), F32),
            vmem((8, DK, BLK), BF16),
            vmem((8, BLK, BLK), F32),
            vmem((8, BLK, BLK), BF16),
            vmem((ROWS, HEADS * DV), F32),
            vmem((ROWS, HEADS * DV), BF16),
            vmem(states, BF16),
            vmem(states, BF16),
            vmem(states, BF16),
            vmem(states, BF16),
            vmem(states, BF16),
            vmem(states, BF16),
            vmem((GROUPS, 8, TILE), F32),
            vmem((18, 8, DV), F32),
            vmem((ROWS, HEADS * DK), F32),
            vmem((ROWS, HEADS * DK), F32),
            vmem((ROWS, HEADS * DV), F32),
            vmem((ROWS, HEADS * DK), BF16),
            vmem((ROWS, HEADS * DK), BF16),
            vmem((ROWS, HEADS * DV), BF16),
            dma((7,)),
            dma((6,)),
            dma((6,)),
            dma((4,)),
            dma((4,)),
            dma((4,)),
            dma((4,)),
            dma((7,)),
            dma((7,)),
            dma((3,)),
        ],
        compiler_params=pltpu.CompilerParams(
            collective_id=0, has_side_effects=True, vmem_limit_bytes=56 * 2**20
        ),
        cost_estimate=pl.CostEstimate(
            flops=7_000_000_000, bytes_accessed=14_000_000, transcendentals=2_000_000
        ),
    )(query, keys, values, out_grad, out_weight, log_decay, block_order)


def solution(mesh):
    placed = (
        P("ctx", "head"),
        P("ctx", "head"),
        P("ctx", "head"),
        P("ctx", "head"),
        P("head", None),
        P("head", "ctx"),
        P(),
    )
    return jax.shard_map(
        on_device,
        mesh=mesh,
        in_specs=placed,
        out_specs=(P("ctx", "head"), P("ctx", "head"), P("ctx", "head")),
        check_vma=False,
    )
```

```python
import jax
import jax.numpy as jnp
from jax import lax
from jax.experimental import pallas as pl
from jax.experimental.pallas import tpu as pltpu
from jax.sharding import PartitionSpec as P

MESH = pl.DeviceIdType.MESH
F32 = jnp.float32
BF16 = jnp.bfloat16
HEADS = 4
DK = 128
DV = 256
BLK = 384
ROWS = 768
COLS = 512
TILE = 128
GROUPS = 32
SCALE = DK ** -0.5

NT = (((1,), (1,)), ((), ()))
NN = (((1,), (0,)), ((), ()))
TN = (((0,), (0,)), ((), ()))


def dot(a, b, dims):
    return lax.dot_general(a, b, dims, preferred_element_type=F32)


def exact_dot(a, b, dims):
    return lax.dot_general(
        a, b, dims, preferred_element_type=F32, precision=lax.Precision.HIGHEST
    )


CHUNKS = ((0, 384), (384, 256), (640, 128))
RELAYS = ((1, 1), (2, 3), (3, 4))


def kernel(
    q_hbm, k_hbm, v_hbm, og_hbm, w_hbm, ld_hbm, bo_hbm,
    dq_hbm, dk_hbm, dv_hbm,
    q, k, v, og, w, ld, bo,
    lrow, lcol, qdec, kdec, qpt, dec, probs,
    part, d_out, m_sum,
    n_own, n_one, n_two, m_own, m_one, m_two, relay,
    totals, total_rows, order_rows, factors, weights, a_sum,
    dq_sum, dk_sum, dv_sum, dq_out, dk_out, dv_out,
    loc_sem, og_ss, og_rs, n_ss, n_rs, m_ss, m_rs, relay_ss, relay_rs, t_ss, t_rs, out_sem,
):
    c = lax.axis_index("ctx")
    p = lax.axis_index("head")
    x = lax.rem(c, 4)
    y = lax.rem(c // 4, 4)
    zh = c // 16
    at16 = lax.rem(c, 16)
    core_mate = p + 1 - 2 * lax.rem(p, 2)
    z_mate = lax.rem(p + 2, 4)
    diag_mate = lax.rem(core_mate + 2, 4)
    later = lax.rem(c + 1, GROUPS)
    earlier = lax.rem(c + GROUPS - 1, GROUPS)
    x_peers = [c - x + lax.rem(x + a, 4) for a in (1, 2, 3)]
    y_peers = [c - 4 * y + 4 * lax.rem(y + a, 4) for a in (1, 2, 3)]
    zh_peer = lax.rem(c + 16, GROUPS)
    last = at16 == 15
    first = at16 == 0

    local = [
        pltpu.make_async_copy(src, dst, loc_sem.at[i])
        for i, (src, dst) in enumerate(
            ((ld_hbm, ld), (bo_hbm, bo), (k_hbm, k), (v_hbm, v), (q_hbm, q),
             (og_hbm, og.at[0]), (w_hbm, w))
        )
    ]
    for copy in local:
        copy.start()
    ld_in, bo_in, k_in, v_in, q_in, og_in, w_in = local

    barrier = pltpu.get_barrier_semaphore()

    def greet(to, who):
        pl.semaphore_signal(barrier, inc=1, device_id=(to, who), device_id_type=MESH)

    partners = [(c, core_mate), (c, z_mate), (later, p), (earlier, p), (zh_peer, p)]
    partners += [(peer, p) for peer in x_peers + y_peers]
    for to, who in partners:
        greet(to, who)
    for _, step in RELAYS:
        pl.when(last)(lambda step=step: greet(later + step, p))
        pl.when(first)(lambda step=step: greet(earlier - step, p))
        pl.when(at16 == step)(lambda step=step: greet(lax.rem(c - step - 1 + GROUPS, GROUPS), p))
        pl.when(at16 == 15 - step)(lambda step=step: greet(lax.rem(c + step + 1, GROUPS), p))
    relaying = sum(
        [((at16 == step) | (at16 == 15 - step)).astype(jnp.int32) for _, step in RELAYS]
    )
    pl.semaphore_wait(
        barrier, len(partners) + 3 * (last | first).astype(jnp.int32) + relaying
    )

    def send(src, dst, ss, rs, to):
        return pltpu.make_async_remote_copy(
            src_ref=src, dst_ref=dst, send_sem=ss, recv_sem=rs, device_id=to, device_id_type=MESH
        )

    def rows_of(b):
        return pl.ds(b * BLK, BLK)

    def chunk_of(i):
        return pl.ds(*CHUNKS[i])

    z_copy = [
        send(og_hbm.at[chunk_of(i)], og.at[2, chunk_of(i)], og_ss.at[i], og_rs.at[i], (c, z_mate))
        for i in range(3)
    ]
    core_copy = [
        send(og_hbm.at[rows_of(b)], og.at[1, rows_of(b)], og_ss.at[3 + b], og_rs.at[3 + b],
             (c, core_mate))
        for b in (0, 1)
    ]
    diag_copy = [
        send(og.at[2, chunk_of(i)], og.at[3, chunk_of(i)], og_ss.at[5 + i], og_rs.at[5 + i],
             (c, core_mate))
        for i in range(3)
    ]
    n_flow = (n_own, n_one, n_two, n_ss, n_rs, later, last, 1)
    m_flow = (m_own, m_one, m_two, m_ss, m_rs, earlier, first, -1)

    def whole(flow, i):
        own, one, two, ss, rs, to, _, _ = flow
        src, dst = (own, one) if i < 2 else (one, two)
        return send(src.at[i % 2], dst.at[i % 2], ss.at[i], rs.at[i], (to, p))

    def start(flow, i):
        own, one, two, ss, rs, to, wraps, sign = flow
        src, dst = (own, one) if i < 2 else (one, two)

        @pl.when(jnp.logical_not(wraps))
        def _():
            whole(flow, i).start()

        @pl.when(wraps)
        def _():
            for h, step in RELAYS:
                send(src.at[i % 2, h], relay.at[i], ss.at[i], relay_rs.at[i],
                     (to + sign * step, p)).start()
            send(src.at[i % 2, 0], dst.at[i % 2, 0], ss.at[i], rs.at[i], (to, p)).start()

    def pass_on(flow, i):
        own, one, two, ss, rs, _, _, sign = flow
        dst = one if i < 2 else two
        for h, step in RELAYS:
            @pl.when(at16 == (step if sign == 1 else 15 - step))
            def _(h=h, step=step):
                copy = send(relay.at[i], dst.at[i % 2, h], relay_ss.at[i], rs.at[i],
                            (c - sign * step, p))
                send(relay.at[i], relay.at[i], relay_ss.at[i], relay_rs.at[i],
                     (c - sign * step, p)).wait_recv()
                copy.start()

    tx_copy = [
        send(totals.at[pl.ds(c, 1)], totals.at[pl.ds(c, 1)], t_ss.at[a], t_rs.at[a], (x_peers[a], p))
        for a in range(3)
    ]
    ty_copy = [
        send(totals.at[pl.ds(c - x, 4)], totals.at[pl.ds(c - x, 4)], t_ss.at[3 + a], t_rs.at[3 + a],
             (y_peers[a], p))
        for a in range(3)
    ]
    tz_copy = send(
        totals.at[pl.ds(zh * 16, 16)], totals.at[pl.ds(zh * 16, 16)], t_ss.at[6], t_rs.at[6],
        (zh_peer, p),
    )

    for copy in z_copy + core_copy:
        copy.start()

    ld_in.wait()
    logs = jnp.concatenate([ld[:, :BLK], ld[:, BLK:]], axis=0)
    up_to = (
        lax.broadcasted_iota(jnp.int32, (BLK, BLK), 0)
        <= lax.broadcasted_iota(jnp.int32, (BLK, BLK), 1)
    ).astype(F32)
    lrow[...] = exact_dot(logs, up_to, NN).reshape(8, 1, BLK)
    total = exact_dot(logs, jnp.ones((BLK, TILE), F32), NN)
    mine = lax.broadcasted_iota(jnp.int32, (8, TILE), 1) // 16 == lax.broadcasted_iota(
        jnp.int32, (8, TILE), 0
    )
    totals[pl.ds(c, 1)] = jnp.sum(jnp.where(mine, total, 0.0), axis=0).reshape(1, 1, TILE)
    for copy in tx_copy:
        copy.start()
    columns = exact_dot(up_to, logs, (((0,), (1,)), ((), ())))
    for j in range(8):
        column = jnp.broadcast_to(columns[:, j : j + 1], (BLK, TILE))
        lcol[j] = column
        qdec[j] = jnp.exp(column)
        kdec[j] = jnp.exp(total[j : j + 1, :] - column)

    def key_cols(h):
        return pl.ds(pl.multiple_of(h * DK, DK), DK)

    def value_cols(h):
        return pl.ds(pl.multiple_of(h * DV, DV), DV)

    k_in.wait()
    v_in.wait()
    for b in (0, 1):
        for h in range(HEADS):
            scaled = (k[rows_of(b), key_cols(h)].astype(F32) * kdec[b * 4 + h]).astype(BF16)
            n_own[b, h] = dot(scaled, v[rows_of(b), value_cols(h)], TN).astype(BF16)
        start(n_flow, b)

    for copy in tx_copy:
        copy.wait_recv()
    for copy in ty_copy:
        copy.start()

    q_in.wait()

    def early_part(b, h):
        j = b * 4 + h
        scaled = (q[rows_of(b), key_cols(h)].astype(F32) * qdec[j]).astype(BF16)
        qpt[j] = jnp.transpose(scaled)
        for i in range(3):
            at = i * TILE
            width = BLK - at
            gap = lrow[j][:, at:] - jnp.concatenate(
                [lcol[j, pl.ds(at, TILE)]] * (width // TILE), axis=1
            )
            on = lax.broadcasted_iota(jnp.int32, (TILE, width), 1) >= lax.broadcasted_iota(
                jnp.int32, (TILE, width), 0
            )
            decay = jnp.where(on, jnp.exp(jnp.minimum(gap, 0.0)), 0.0) * SCALE
            dec[j, pl.ds(at, TILE), pl.ds(at, width)] = decay
            scores = dot(
                k[pl.ds(b * BLK + at, TILE), key_cols(h)],
                q[pl.ds(b * BLK + at, width), key_cols(h)],
                NT,
            )
            probs[j, pl.ds(at, TILE), pl.ds(at, width)] = (scores * decay).astype(BF16)

    lax.fori_loop(0, HEADS, lambda h, _: (early_part(0, h), 0)[1], 0)
    for copy in ty_copy:
        copy.wait_recv()
    tz_copy.start()
    lax.fori_loop(0, HEADS, lambda h, _: (early_part(1, h), 0)[1], 0)

    def product(slot, owner, rows):
        return dot(
            og[slot, rows], w[:, pl.ds(pl.multiple_of(owner * COLS, COLS), COLS)], NT
        )

    og_in.wait()
    w_in.wait()
    for b in (0, 1):
        core_copy[b].wait_recv()
        part[rows_of(b)] = product(0, p, rows_of(b)) + product(1, core_mate, rows_of(b))

    def late_part(b, h):
        j = b * 4 + h
        for i in range(3):
            at = i * TILE
            width = BLK - at
            s_rows = pl.ds(b * BLK + at, TILE)
            t_rows = pl.ds(b * BLK + at, width)
            grads = d_out[t_rows, value_cols(h)]
            scores = dot(v[s_rows, value_cols(h)], grads, NT)
            grad_weights = (scores * dec[j, pl.ds(at, TILE), pl.ds(at, width)]).astype(BF16)
            dv_sum[s_rows, value_cols(h)] = dot(
                probs[j, pl.ds(at, TILE), pl.ds(at, width)], grads, NN
            )
            dk_sum[s_rows, key_cols(h)] = dot(grad_weights, q[t_rows, key_cols(h)], NN)
            to_query = dot(grad_weights, k[s_rows, key_cols(h)], TN)
            if i == 0:
                dq_sum[t_rows, key_cols(h)] = to_query
            else:
                dq_sum[t_rows, key_cols(h)] += to_query

    def gather(i):
        rows = chunk_of(i)
        z_copy[i].wait_recv()
        diag_copy[i].start()
        part[rows] += product(2, z_mate, rows)
        diag_copy[i].wait_recv()
        d_out[rows] = (part[rows] + product(3, diag_mate, rows)).astype(BF16)

    gather(0)
    for h in range(HEADS):
        m_own[0, h] = dot(qpt[h], d_out[rows_of(0), value_cols(h)], NN).astype(BF16)
    start(m_flow, 0)

    @pl.when(jnp.logical_not(first))
    def _():
        whole(n_flow, 0).wait_recv()

    @pl.when(jnp.logical_not(first | last))
    def _():
        whole(n_flow, 2).start()

    lax.fori_loop(0, HEADS, lambda h, _: (late_part(0, h), 0)[1], 0)

    @pl.when(jnp.logical_not(first))
    def _():
        whole(n_flow, 1).wait_recv()

    @pl.when(jnp.logical_not(first | last))
    def _():
        whole(n_flow, 3).start()

    pass_on(n_flow, 0)
    pass_on(n_flow, 1)

    tz_copy.wait_recv()
    bo_in.wait()

    def place(group, b):
        return bo[2 * group + b]

    own = [place(c, b) for b in (0, 1)]
    late = [place(lax.rem(c + d, GROUPS), b) for d in (1, 2) for b in (0, 1)]
    early = [place(lax.rem(c + GROUPS - d, GROUPS), b) for d in (1, 2) for b in (0, 1)]
    pairs = [(o, own[b]) for b in (0, 1) for o in [own[1 - b]] + late]
    pairs += [(own[b], o) for b in (0, 1) for o in early]
    first_half = lax.broadcasted_iota(jnp.int32, (1, TILE), 1) < 64
    for g in range(GROUPS):
        total_rows[g : g + 1] = totals[g]
        order_rows[g : g + 1] = jnp.where(first_half, bo[2 * g], bo[2 * g + 1])
    for n, (hi, lo) in enumerate(pairs):
        at = order_rows[...]
        gap = jnp.sum(
            jnp.where((at > lo) & (at < hi), total_rows[...], 0.0), axis=0, keepdims=True
        )
        gap = gap + jnp.concatenate([gap[:, 64:], gap[:, :64]], axis=1)
        seen = jnp.full((1, TILE), hi, jnp.int32) > lo
        factors[n : n + 1] = jnp.where(seen, jnp.exp(gap), 0.0) * SCALE
    for h in range(HEADS):
        weights[h] = jnp.broadcast_to(factors[:, h * 16 : h * 16 + 1], (24, DV))

    def weighted(n, state, h):
        return weights[h, n : n + 1] * state.astype(F32)

    gather(1)
    for h in range(HEADS):
        m_sum[h] = dot(qpt[4 + h, :, :256], d_out[chunk_of(1), value_cols(h)], NN)
    gather(2)
    for h in range(HEADS):
        m_own[1, h] = (
            m_sum[h] + dot(qpt[4 + h, :, 256:], d_out[chunk_of(2), value_cols(h)], NN)
        ).astype(BF16)
    start(m_flow, 1)

    @pl.when(last)
    def _():
        start(n_flow, 2)
        start(n_flow, 3)

    @pl.when(first)
    def _():
        whole(n_flow, 0).wait_recv()
        whole(n_flow, 2).start()
        whole(n_flow, 1).wait_recv()
        whole(n_flow, 3).start()

    pass_on(m_flow, 0)

    @pl.when(jnp.logical_not(last))
    def _():
        whole(m_flow, 0).wait_recv()
        start(m_flow, 2)

    lax.fori_loop(0, HEADS, lambda h, _: (late_part(1, h), 0)[1], 0)
    pass_on(n_flow, 2)
    pass_on(n_flow, 3)
    pass_on(m_flow, 1)

    @pl.when(last)
    def _():
        whole(m_flow, 0).wait_recv()
        whole(m_flow, 2).start()

    whole(n_flow, 2).wait_recv()
    whole(n_flow, 3).wait_recv()
    for b in (0, 1):
        for h in range(HEADS):
            state = weighted(5 * (1 - b), n_own[1 - b, h], h)
            for i, source in enumerate((n_one, n_two)):
                for other in (0, 1):
                    state = state + weighted(10 + 4 * b + 2 * i + other, source[other, h], h)
            rest = dot(d_out[rows_of(b), value_cols(h)], state.astype(BF16), NT)
            dq_out[rows_of(b), key_cols(h)] = (
                dq_sum[rows_of(b), key_cols(h)] + rest * qdec[b * 4 + h]
            ).astype(BF16)
    dq_done = pltpu.make_async_copy(dq_out, dq_hbm, out_sem.at[0])
    dq_done.start()

    pass_on(m_flow, 2)
    whole(m_flow, 1).wait_recv()
    start(m_flow, 3)
    pass_on(m_flow, 3)
    whole(m_flow, 2).wait_recv()
    for b in (0, 1):
        for h in range(HEADS):
            state = weighted(5 * b, m_own[1 - b, h], h)
            for n, source in ((1, m_one[0, h]), (2, m_one[1, h]), (3, m_two[0, h])):
                state = state + weighted(5 * b + n, source, h)
            a_sum[b, h] = state
    whole(m_flow, 3).wait_recv()
    done = [dq_done]
    for b in (0, 1):
        for h in range(HEADS):
            state = (a_sum[b, h] + weighted(5 * b + 4, m_two[1, h], h)).astype(BF16)
            decay = kdec[b * 4 + h]
            to_value = dot(k[rows_of(b), key_cols(h)], state, NN)
            to_key = dot(v[rows_of(b), value_cols(h)], state, NT)
            dv_out[rows_of(b), value_cols(h)] = (
                dv_sum[rows_of(b), value_cols(h)]
                + to_value * jnp.concatenate([decay, decay], axis=1)
            ).astype(BF16)
            dk_out[rows_of(b), key_cols(h)] = (
                dk_sum[rows_of(b), key_cols(h)] + to_key * decay
            ).astype(BF16)
        done.append(
            pltpu.make_async_copy(dk_out.at[rows_of(b)], dk_hbm.at[rows_of(b)], out_sem.at[1 + b])
        )
        done.append(
            pltpu.make_async_copy(dv_out.at[rows_of(b)], dv_hbm.at[rows_of(b)], out_sem.at[3 + b])
        )
        done[-2].start()
        done[-1].start()
    for copy in z_copy + core_copy + diag_copy:
        copy.wait_send()
    for i in range(4):
        whole(n_flow, i).wait_send()
        whole(m_flow, i).wait_send()

        @pl.when(relaying > 0)
        def _(i=i):
            send(relay.at[i], relay.at[i], relay_ss.at[i], relay_rs.at[i],
                 (later, p)).wait_send()

    for copy in tx_copy + ty_copy + [tz_copy]:
        copy.wait_send()
    for copy in done:
        copy.wait()


def on_device(query, keys, values, out_grad, out_weight, log_decay, block_order):
    anywhere = pl.BlockSpec(memory_space=pl.ANY)
    vmem = pltpu.VMEM
    states = (2, HEADS, DK, DV)
    dma = pltpu.SemaphoreType.DMA
    return pl.pallas_call(
        kernel,
        name="retention_backward",
        out_shape=(
            jax.ShapeDtypeStruct((ROWS, HEADS * DK), BF16),
            jax.ShapeDtypeStruct((ROWS, HEADS * DK), BF16),
            jax.ShapeDtypeStruct((ROWS, HEADS * DV), BF16),
        ),
        in_specs=[anywhere] * 7,
        out_specs=(anywhere,) * 3,
        scratch_shapes=[
            vmem((ROWS, HEADS * DK), BF16),
            vmem((ROWS, HEADS * DK), BF16),
            vmem((ROWS, HEADS * DV), BF16),
            vmem((4, ROWS, COLS), BF16),
            vmem((HEADS * DV, 4 * COLS), BF16),
            vmem((HEADS, ROWS), F32),
            pltpu.SMEM((2 * GROUPS,), jnp.int32),
            vmem((8, 1, BLK), F32),
            vmem((8, BLK, TILE), F32),
            vmem((8, BLK, TILE), F32),
            vmem((8, BLK, TILE), F32),
            vmem((8, DK, BLK), BF16),
            vmem((8, BLK, BLK), F32),
            vmem((8, BLK, BLK), BF16),
            vmem((ROWS, HEADS * DV), F32),
            vmem((ROWS, HEADS * DV), BF16),
            vmem((HEADS, DK, DV), F32),
            vmem(states, BF16),
            vmem(states, BF16),
            vmem(states, BF16),
            vmem(states, BF16),
            vmem(states, BF16),
            vmem(states, BF16),
            vmem((4, DK, DV), BF16),
            vmem((GROUPS, 1, TILE), F32),
            vmem((GROUPS, TILE), F32),
            vmem((GROUPS, TILE), jnp.int32),
            vmem((24, TILE), F32),
            vmem((HEADS, 24, DV), F32),
            vmem(states, F32),
            vmem((ROWS, HEADS * DK), F32),
            vmem((ROWS, HEADS * DK), F32),
            vmem((ROWS, HEADS * DV), F32),
            vmem((ROWS, HEADS * DK), BF16),
            vmem((ROWS, HEADS * DK), BF16),
            vmem((ROWS, HEADS * DV), BF16),
            dma((7,)),
            dma((8,)),
            dma((8,)),
            dma((4,)),
            dma((4,)),
            dma((4,)),
            dma((4,)),
            dma((4,)),
            dma((4,)),
            dma((7,)),
            dma((7,)),
            dma((5,)),
        ],
        compiler_params=pltpu.CompilerParams(
            collective_id=0, has_side_effects=True, vmem_limit_bytes=56 * 2**20
        ),
        cost_estimate=pl.CostEstimate(
            flops=7_000_000_000, bytes_accessed=14_000_000, transcendentals=2_000_000
        ),
    )(query, keys, values, out_grad, out_weight, log_decay, block_order)


def solution(mesh):
    placed = (
        P("ctx", "head"),
        P("ctx", "head"),
        P("ctx", "head"),
        P("ctx", "head"),
        P("head", None),
        P("head", "ctx"),
        P(),
    )
    return jax.shard_map(
        on_device,
        mesh=mesh,
        in_specs=placed,
        out_specs=(P("ctx", "head"), P("ctx", "head"), P("ctx", "head")),
        check_vma=False,
    )
```

```python
import jax
import jax.numpy as jnp
from jax import lax
from jax.experimental import pallas as pl
from jax.experimental.pallas import tpu as pltpu
from jax.sharding import PartitionSpec as P

MESH = pl.DeviceIdType.MESH
F32 = jnp.float32
BF16 = jnp.bfloat16
HEADS = 4
DK = 128
DV = 256
BLK = 384
ROWS = 768
COLS = 512
TILE = 128
GROUPS = 32
SCALE = DK ** -0.5

NT = (((1,), (1,)), ((), ()))
NN = (((1,), (0,)), ((), ()))
TN = (((0,), (0,)), ((), ()))


def dot(a, b, dims):
    return lax.dot_general(a, b, dims, preferred_element_type=F32)


def exact_dot(a, b, dims):
    return lax.dot_general(
        a, b, dims, preferred_element_type=F32, precision=lax.Precision.HIGHEST
    )


PIECES = 6
RELAYS = ((1, 1), (2, 3), (3, 4))
PASS_RELAYS = ((0, 3), (1, 4))
CHAINED = {1: (2, 2), -1: (2, 2)}


def kernel(
    q_hbm, k_hbm, v_hbm, og_hbm, w_hbm, ld_hbm, bo_hbm,
    dq_hbm, dk_hbm, dv_hbm,
    q, k, v, og, w, ld, bo,
    lrow, lcol, qdec, kdec, qpt, dec, probs,
    part, d_out, m_sum,
    n_own, n_one, n_two, n_via, m_own, m_one, m_two, m_via, relay,
    totals, total_rows, order_rows, factors, weights, a_sum,
    dq_sum, dk_sum, dv_sum, dq_out, dk_out, dv_out,
    loc_sem, og_ss, og_rs, n_ss, n_rs, m_ss, m_rs, relay_ss, relay_rs, t_ss, t_rs, out_sem,
):
    c = lax.axis_index("ctx")
    p = lax.axis_index("head")
    x = lax.rem(c, 4)
    y = lax.rem(c // 4, 4)
    zh = c // 16
    at16 = lax.rem(c, 16)
    core_mate = p + 1 - 2 * lax.rem(p, 2)
    z_mate = lax.rem(p + 2, 4)
    diag_mate = lax.rem(core_mate + 2, 4)
    later = lax.rem(c + 1, GROUPS)
    earlier = lax.rem(c + GROUPS - 1, GROUPS)
    x_peers = [c - x + lax.rem(x + a, 4) for a in (1, 2, 3)]
    y_peers = [c - 4 * y + 4 * lax.rem(y + a, 4) for a in (1, 2, 3)]
    zh_peer = lax.rem(c + 16, GROUPS)
    last = at16 == 15
    first = at16 == 0

    def beside(group, step):
        column = lax.rem(group, 4)
        return group - column + lax.rem(column + step, 4)

    right, left = beside(c, 1), beside(c, 3)
    n_target = lax.rem(right + 2, GROUPS)
    m_target = lax.rem(left + GROUPS - 2, GROUPS)
    n_helper = beside(lax.rem(c + GROUPS - 2, GROUPS), 3)
    m_helper = beside(lax.rem(c + 2, GROUPS), 1)

    local = [
        pltpu.make_async_copy(src, dst, loc_sem.at[i])
        for i, (src, dst) in enumerate(
            ((ld_hbm, ld), (bo_hbm, bo), (k_hbm, k), (v_hbm, v), (q_hbm, q),
             (og_hbm, og.at[0]), (w_hbm, w))
        )
    ]
    for copy in local:
        copy.start()
    ld_in, bo_in, k_in, v_in, q_in, og_in, w_in = local

    barrier = pltpu.get_barrier_semaphore()

    def greet(to, who):
        pl.semaphore_signal(barrier, inc=1, device_id=(to, who), device_id_type=MESH)

    partners = [(c, core_mate), (c, z_mate), (later, p), (earlier, p), (zh_peer, p)]
    partners += [(peer, p) for peer in x_peers + y_peers]
    partners += [(to, p) for to in (n_target, m_target, n_helper, m_helper)]
    for to, who in partners:
        greet(to, who)
    for _, step in RELAYS:
        pl.when(last)(lambda step=step: greet(later + step, p))
        pl.when(first)(lambda step=step: greet(earlier - step, p))
        pl.when(at16 == step)(lambda step=step: greet(lax.rem(c - step - 1 + GROUPS, GROUPS), p))
        pl.when(at16 == 15 - step)(lambda step=step: greet(lax.rem(c + step + 1, GROUPS), p))
    relaying = sum(
        [((at16 == step) | (at16 == 15 - step)).astype(jnp.int32) for _, step in RELAYS]
    )
    next_only = ((at16 == 1) | (at16 == 14)).astype(jnp.int32)
    pl.semaphore_wait(
        barrier, len(partners) + 3 * (last | first).astype(jnp.int32) + relaying
    )

    def send(src, dst, ss, rs, to):
        return pltpu.make_async_remote_copy(
            src_ref=src, dst_ref=dst, send_sem=ss, recv_sem=rs, device_id=to, device_id_type=MESH
        )

    def rows_of(b):
        return pl.ds(b * BLK, BLK)

    def piece_of(i):
        return pl.ds(i * TILE, TILE)

    z_copy = [
        send(og_hbm.at[piece_of(i)], og.at[2, piece_of(i)], og_ss.at[i], og_rs.at[i], (c, z_mate))
        for i in range(PIECES)
    ]
    diag_copy = [
        send(og.at[2, piece_of(i)], og.at[3, piece_of(i)], og_ss.at[PIECES + i],
             og_rs.at[PIECES + i], (c, core_mate))
        for i in range(PIECES)
    ]
    core_copy = [
        send(og_hbm.at[rows_of(b)], og.at[1, rows_of(b)], og_ss.at[2 * PIECES + b],
             og_rs.at[2 * PIECES + b], (c, core_mate))
        for b in (0, 1)
    ]
    n_flow = (n_own, n_one, n_two, n_via, n_ss, n_rs, later, left, n_target, 1)
    m_flow = (m_own, m_one, m_two, m_via, m_ss, m_rs, earlier, right, m_target, -1)

    def wraps(sign):
        return last if sign == 1 else first

    def half(h):
        return pl.ds(2 * h, 2)

    def first_hop(flow, b, h):
        own, one, _, _, ss, rs, to, _, _, _ = flow
        return send(own.at[b, half(h)], one.at[b, half(h)], ss.at[2 * b + h], rs.at[2 * b + h], (to, p))

    def chained(flow, b):
        return CHAINED[flow[-1]][b]

    def second_hop(flow, b):
        _, one, two, _, ss, rs, to, _, _, _ = flow
        heads = pl.ds(0, chained(flow, b))
        return send(one.at[b, heads], two.at[b, heads], ss.at[4 + b], rs.at[4 + b], (to, p))

    def both_arrive(flow, b):
        _, one, two, _, ss, rs, to, _, _, _ = flow
        return send(one.at[b], two.at[b], ss.at[4 + b], rs.at[4 + b], (to, p))

    def side_hop(flow, b):
        own, _, _, via, ss, rs, _, to, _, _ = flow
        k = chained(flow, b)
        return send(own.at[b, pl.ds(k, HEADS - k)], via.at[b, pl.ds(0, HEADS - k)],
                    ss.at[6 + b], rs.at[6 + b], (to, p))

    def side_second_hop(flow, b):
        _, _, two, via, ss, rs, _, _, to, _ = flow
        k = chained(flow, b)
        return send(via.at[b, pl.ds(0, HEADS - k)], two.at[b, pl.ds(k, HEADS - k)],
                    ss.at[8 + b], rs.at[4 + b], (to, p))

    def to_relays(flow, b, h):
        own, one, _, _, ss, rs, to, _, _, sign = flow
        for n in (2 * h, 2 * h + 1):
            if n == 0:
                send(own.at[b, n], one.at[b, n], ss.at[2 * b], rs.at[2 * b], (to, p)).start()
            else:
                send(own.at[b, n], relay.at[b], ss.at[2 * b + h], relay_rs.at[b],
                     (to + sign * RELAYS[n - 1][1], p)).start()

    def start(flow, b, h):
        @pl.when(jnp.logical_not(wraps(flow[-1])))
        def _():
            first_hop(flow, b, h).start()

        @pl.when(wraps(flow[-1]))
        def _():
            to_relays(flow, b, h)

        if h == 0 and chained(flow, b) < HEADS:
            side_hop(flow, b).start()

    def pass_chain(flow, b):
        _, one, two, _, ss, rs, to, _, _, sign = flow
        k = chained(flow, b)
        first_hop(flow, b, 0).wait_recv()
        if k > 2:
            first_hop(flow, b, 1).wait_recv()

        @pl.when(jnp.logical_not(wraps(sign)))
        def _():
            second_hop(flow, b).start()

        @pl.when(wraps(sign))
        def _():
            for n, step in PASS_RELAYS:
                send(one.at[b, n], relay.at[2 + b], ss.at[4 + b], relay_rs.at[2 + b],
                     (to + sign * step, p)).start()
            if k > 2:
                heads = pl.ds(2, k - 2)
                send(one.at[b, heads], two.at[b, heads], ss.at[4 + b], rs.at[4 + b],
                     (to, p)).start()

    def pass_side(flow, b):
        if chained(flow, b) < HEADS:
            side_hop(flow, b).wait_recv()
            side_second_hop(flow, b).start()

    def pass_relay(flow, slot):
        _, one, two, _, _, rs, _, _, _, sign = flow
        b = slot % 2
        for n, step in RELAYS if slot < 2 else PASS_RELAYS:
            @pl.when(at16 == (step if sign == 1 else 15 - step))
            def _(n=n, step=step):
                to = (c - sign * step, p)
                sem = 2 * b + n // 2 if slot < 2 else 4 + b
                send(relay.at[slot], relay.at[slot], relay_ss.at[slot], relay_rs.at[slot],
                     to).wait_recv()
                send(relay.at[slot], (one if slot < 2 else two).at[b, n], relay_ss.at[slot],
                     rs.at[sem], to).start()

    def sent(flow, b):
        first_hop(flow, b, 0).wait_send()
        first_hop(flow, b, 1).wait_send()
        second_hop(flow, b).wait_send()
        if chained(flow, b) < HEADS:
            side_hop(flow, b).wait_send()
            side_second_hop(flow, b).wait_send()

    tx_copy = [
        send(totals.at[pl.ds(c, 1)], totals.at[pl.ds(c, 1)], t_ss.at[a], t_rs.at[a], (x_peers[a], p))
        for a in range(3)
    ]
    ty_copy = [
        send(totals.at[pl.ds(c - x, 4)], totals.at[pl.ds(c - x, 4)], t_ss.at[3 + a], t_rs.at[3 + a],
             (y_peers[a], p))
        for a in range(3)
    ]
    tz_copy = send(
        totals.at[pl.ds(zh * 16, 16)], totals.at[pl.ds(zh * 16, 16)], t_ss.at[6], t_rs.at[6],
        (zh_peer, p),
    )

    for copy in core_copy + z_copy[:3]:
        copy.start()

    ld_in.wait()
    logs = jnp.concatenate([ld[:, :BLK], ld[:, BLK:]], axis=0)
    up_to = (
        lax.broadcasted_iota(jnp.int32, (BLK, BLK), 0)
        <= lax.broadcasted_iota(jnp.int32, (BLK, BLK), 1)
    ).astype(F32)
    lrow[...] = exact_dot(logs, up_to, NN).reshape(8, 1, BLK)
    total = exact_dot(logs, jnp.ones((BLK, TILE), F32), NN)
    mine = lax.broadcasted_iota(jnp.int32, (8, TILE), 1) // 16 == lax.broadcasted_iota(
        jnp.int32, (8, TILE), 0
    )
    totals[pl.ds(c, 1)] = jnp.sum(jnp.where(mine, total, 0.0), axis=0).reshape(1, 1, TILE)
    for copy in tx_copy:
        copy.start()
    columns = exact_dot(up_to, logs, (((0,), (1,)), ((), ())))
    for j in range(8):
        column = jnp.broadcast_to(columns[:, j : j + 1], (BLK, TILE))
        lcol[j] = column
        qdec[j] = jnp.exp(column)
        kdec[j] = jnp.exp(total[j : j + 1, :] - column)

    def key_cols(h):
        return pl.ds(pl.multiple_of(h * DK, DK), DK)

    def value_cols(h):
        return pl.ds(pl.multiple_of(h * DV, DV), DV)

    k_in.wait()
    v_in.wait()
    for b in (0, 1):
        for h in range(HEADS):
            scaled = (k[rows_of(b), key_cols(h)].astype(F32) * kdec[b * 4 + h]).astype(BF16)
            n_own[b, h] = dot(scaled, v[rows_of(b), value_cols(h)], TN).astype(BF16)
        start(n_flow, b, 0)
        start(n_flow, b, 1)

    q_in.wait()

    def early_part(b, h):
        j = b * 4 + h
        scaled = (q[rows_of(b), key_cols(h)].astype(F32) * qdec[j]).astype(BF16)
        qpt[j] = jnp.transpose(scaled)
        for i in range(3):
            at = i * TILE
            width = BLK - at
            gap = lrow[j][:, at:] - jnp.concatenate(
                [lcol[j, pl.ds(at, TILE)]] * (width // TILE), axis=1
            )
            on = lax.broadcasted_iota(jnp.int32, (TILE, width), 1) >= lax.broadcasted_iota(
                jnp.int32, (TILE, width), 0
            )
            decay = jnp.where(on, jnp.exp(jnp.minimum(gap, 0.0)), 0.0) * SCALE
            dec[j, pl.ds(at, TILE), pl.ds(at, width)] = decay
            scores = dot(
                k[pl.ds(b * BLK + at, TILE), key_cols(h)],
                q[pl.ds(b * BLK + at, width), key_cols(h)],
                NT,
            )
            probs[j, pl.ds(at, TILE), pl.ds(at, width)] = (scores * decay).astype(BF16)

    for j in range(8):
        early_part(j // 4, j % 4)
    for copy in z_copy[3:]:
        copy.start()

    def product(slot, owner, rows):
        return dot(
            og[slot, rows], w[:, pl.ds(pl.multiple_of(owner * COLS, COLS), COLS)], NT
        )

    og_in.wait()
    w_in.wait()
    for b in (0, 1):
        core_copy[b].wait_recv()
        part[rows_of(b)] = product(0, p, rows_of(b)) + product(1, core_mate, rows_of(b))

    def late_part(b, h):
        j = b * 4 + h
        for i in range(3):
            at = i * TILE
            width = BLK - at
            s_rows = pl.ds(b * BLK + at, TILE)
            t_rows = pl.ds(b * BLK + at, width)
            grads = d_out[t_rows, value_cols(h)]
            scores = dot(v[s_rows, value_cols(h)], grads, NT)
            grad_weights = (scores * dec[j, pl.ds(at, TILE), pl.ds(at, width)]).astype(BF16)
            dv_sum[s_rows, value_cols(h)] = dot(
                probs[j, pl.ds(at, TILE), pl.ds(at, width)], grads, NN
            )
            dk_sum[s_rows, key_cols(h)] = dot(grad_weights, q[t_rows, key_cols(h)], NN)
            to_query = dot(grad_weights, k[s_rows, key_cols(h)], TN)
            if i == 0:
                dq_sum[t_rows, key_cols(h)] = to_query
            else:
                dq_sum[t_rows, key_cols(h)] += to_query

    def gather(first_piece, pieces):
        for i in range(first_piece, first_piece + pieces):
            z_copy[i].wait_recv()
            diag_copy[i].start()
        rows = pl.ds(first_piece * TILE, pieces * TILE)
        part[rows] += product(2, z_mate, rows)
        for i in range(first_piece, first_piece + pieces):
            diag_copy[i].wait_recv()
        d_out[rows] = (part[rows] + product(3, diag_mate, rows)).astype(BF16)

    n_aside = (at16 != 13) & (at16 != 14)

    @pl.when(n_aside)
    def _():
        pass_side(n_flow, 0)
        pass_side(n_flow, 1)

    for copy in tx_copy:
        copy.wait_recv()
    for copy in ty_copy:
        copy.start()
    gather(0, 3)
    for h in range(HEADS):
        m_own[0, h] = dot(qpt[h], d_out[rows_of(0), value_cols(h)], NN).astype(BF16)
    start(m_flow, 0, 0)

    @pl.when(jnp.logical_not(first))
    def _():
        pass_chain(n_flow, 0)

    for h in range(HEADS):
        late_part(0, h)
    start(m_flow, 0, 1)
    for copy in ty_copy:
        copy.wait_recv()
    tz_copy.start()

    @pl.when(jnp.logical_not(first))
    def _():
        pass_chain(n_flow, 1)

    pass_relay(n_flow, 0)
    pass_relay(n_flow, 1)

    def weighted(n, state, h):
        return weights[h, n : n + 1] * state.astype(F32)

    gather(3, 2)
    for h in range(HEADS):
        m_sum[h] = dot(qpt[4 + h, :, :256], d_out[pl.ds(BLK, 256), value_cols(h)], NN)
    gather(5, 1)
    for h in range(HEADS):
        m_own[1, h] = (
            m_sum[h] + dot(qpt[4 + h, :, 256:], d_out[piece_of(5), value_cols(h)], NN)
        ).astype(BF16)
    start(m_flow, 1, 0)
    start(m_flow, 1, 1)
    pass_side(m_flow, 0)
    pass_relay(m_flow, 0)

    @pl.when(jnp.logical_not(last))
    def _():
        pass_chain(m_flow, 0)

    for h in range(HEADS):
        late_part(1, h)

    @pl.when(last)
    def _():
        pass_chain(m_flow, 0)


    @pl.when(jnp.logical_not(n_aside))
    def _():
        pass_side(n_flow, 0)
        pass_side(n_flow, 1)

    @pl.when(first)
    def _():
        pass_chain(n_flow, 0)
        pass_chain(n_flow, 1)

    pass_side(m_flow, 1)
    pass_relay(m_flow, 1)
    pass_chain(m_flow, 1)
    pass_relay(n_flow, 2)
    pass_relay(n_flow, 3)
    pass_relay(m_flow, 2)
    tz_copy.wait_recv()
    bo_in.wait()

    def place(group, b):
        return bo[2 * group + b]

    own = [place(c, b) for b in (0, 1)]
    late = [place(lax.rem(c + d, GROUPS), b) for d in (1, 2) for b in (0, 1)]
    early = [place(lax.rem(c + GROUPS - d, GROUPS), b) for d in (1, 2) for b in (0, 1)]
    pairs = [(o, own[b]) for b in (0, 1) for o in [own[1 - b]] + late]
    pairs += [(own[b], o) for b in (0, 1) for o in early]
    first_half = lax.broadcasted_iota(jnp.int32, (1, TILE), 1) < 64
    for g in range(GROUPS):
        total_rows[g : g + 1] = totals[g]
        order_rows[g : g + 1] = jnp.where(first_half, bo[2 * g], bo[2 * g + 1])
    for n, (hi, lo) in enumerate(pairs):
        at = order_rows[...]
        gap = jnp.sum(
            jnp.where((at > lo) & (at < hi), total_rows[...], 0.0), axis=0, keepdims=True
        )
        gap = gap + jnp.concatenate([gap[:, 64:], gap[:, :64]], axis=1)
        seen = jnp.full((1, TILE), hi, jnp.int32) > lo
        factors[n : n + 1] = jnp.where(seen, jnp.exp(gap), 0.0) * SCALE
    for h in range(HEADS):
        weights[h] = jnp.broadcast_to(factors[:, h * 16 : h * 16 + 1], (24, DV))

    dq_done = pltpu.make_async_copy(dq_out, dq_hbm, out_sem.at[0])

    def finish_query():
        for b in (0, 1):
            if chained(n_flow, b) <= 2:
                first_hop(n_flow, b, 1).wait_recv()
            both_arrive(n_flow, b).wait_recv()
        for b in (0, 1):
            for h in range(HEADS):
                state = weighted(5 * (1 - b), n_own[1 - b, h], h)
                for i, source in enumerate((n_one, n_two)):
                    for other in (0, 1):
                        state = state + weighted(10 + 4 * b + 2 * i + other, source[other, h], h)
                rest = dot(d_out[rows_of(b), value_cols(h)], state.astype(BF16), NT)
                dq_out[rows_of(b), key_cols(h)] = (
                    dq_sum[rows_of(b), key_cols(h)] + rest * qdec[b * 4 + h]
                ).astype(BF16)
        dq_done.start()

    query_last = at16 <= 1
    pl.when(jnp.logical_not(query_last))(finish_query)

    pass_relay(m_flow, 3)
    for b in (0, 1):
        if chained(m_flow, b) <= 2:
            first_hop(m_flow, b, 1).wait_recv()
    both_arrive(m_flow, 0).wait_recv()
    for b in (0, 1):
        for h in range(HEADS):
            state = weighted(5 * b, m_own[1 - b, h], h)
            for n, source in ((1, m_one[0, h]), (2, m_one[1, h]), (3, m_two[0, h])):
                state = state + weighted(5 * b + n, source, h)
            a_sum[b, h] = state
    both_arrive(m_flow, 1).wait_recv()
    done = [dq_done]
    for b in (0, 1):
        for h in range(HEADS):
            state = (a_sum[b, h] + weighted(5 * b + 4, m_two[1, h], h)).astype(BF16)
            decay = kdec[b * 4 + h]
            to_value = dot(k[rows_of(b), key_cols(h)], state, NN)
            to_key = dot(v[rows_of(b), value_cols(h)], state, NT)
            dv_out[rows_of(b), value_cols(h)] = (
                dv_sum[rows_of(b), value_cols(h)]
                + to_value * jnp.concatenate([decay, decay], axis=1)
            ).astype(BF16)
            dk_out[rows_of(b), key_cols(h)] = (
                dk_sum[rows_of(b), key_cols(h)] + to_key * decay
            ).astype(BF16)
        done.append(
            pltpu.make_async_copy(dk_out.at[rows_of(b)], dk_hbm.at[rows_of(b)], out_sem.at[1 + b])
        )
        done.append(
            pltpu.make_async_copy(dv_out.at[rows_of(b)], dv_hbm.at[rows_of(b)], out_sem.at[3 + b])
        )
        done[-2].start()
        done[-1].start()
    pl.when(query_last)(finish_query)
    for copy in z_copy + core_copy + diag_copy:
        copy.wait_send()
    for b in (0, 1):
        sent(n_flow, b)
        sent(m_flow, b)

    for slot in range(4):
        @pl.when(relaying > (0 if slot < 2 else next_only))
        def _(slot=slot):
            send(relay.at[slot], relay.at[slot], relay_ss.at[slot], relay_rs.at[slot],
                 (later, p)).wait_send()

    for copy in tx_copy + ty_copy + [tz_copy]:
        copy.wait_send()
    for copy in done:
        copy.wait()


def hand_over(a, b, d, a_out, b_out, d_out, a_in, b_in, d_in, in_sems, out_sems):
    parts = [
        (array, held, out, pl.ds(n * BLK, BLK))
        for array, held, out in ((d, d_in, d_out), (a, a_in, a_out), (b, b_in, b_out))
        for n in (0, 1)
    ]
    ins = [
        pltpu.make_async_copy(array.at[rows], held.at[rows], in_sems.at[i])
        for i, (array, held, _, rows) in enumerate(parts)
    ]
    outs = [
        pltpu.make_async_copy(held.at[rows], out.at[rows], out_sems.at[i])
        for i, (_, held, out, rows) in enumerate(parts)
    ]
    for copy in ins:
        copy.start()
    for come, go in zip(ins, outs):
        come.wait()
        go.start()
    for copy in outs:
        copy.wait()


def on_device(query, keys, values, out_grad, out_weight, log_decay, block_order):
    anywhere = pl.BlockSpec(memory_space=pl.ANY)
    vmem = pltpu.VMEM
    states = (2, HEADS, DK, DV)
    dma = pltpu.SemaphoreType.DMA
    grads = pl.pallas_call(
        kernel,
        name="retention_backward",
        out_shape=(
            jax.ShapeDtypeStruct((ROWS, HEADS * DK), BF16),
            jax.ShapeDtypeStruct((ROWS, HEADS * DK), BF16),
            jax.ShapeDtypeStruct((ROWS, HEADS * DV), BF16),
        ),
        in_specs=[anywhere] * 7,
        out_specs=(anywhere,) * 3,
        scratch_shapes=[
            vmem((ROWS, HEADS * DK), BF16),
            vmem((ROWS, HEADS * DK), BF16),
            vmem((ROWS, HEADS * DV), BF16),
            vmem((4, ROWS, COLS), BF16),
            vmem((HEADS * DV, 4 * COLS), BF16),
            vmem((HEADS, ROWS), F32),
            pltpu.SMEM((2 * GROUPS,), jnp.int32),
            vmem((8, 1, BLK), F32),
            vmem((8, BLK, TILE), F32),
            vmem((8, BLK, TILE), F32),
            vmem((8, BLK, TILE), F32),
            vmem((8, DK, BLK), BF16),
            vmem((8, BLK, BLK), F32),
            vmem((8, BLK, BLK), BF16),
            vmem((ROWS, HEADS * DV), F32),
            vmem((ROWS, HEADS * DV), BF16),
            vmem((HEADS, DK, DV), F32),
            vmem(states, BF16),
            vmem(states, BF16),
            vmem(states, BF16),
            vmem((2, HEADS, DK, DV), BF16),
            vmem(states, BF16),
            vmem(states, BF16),
            vmem(states, BF16),
            vmem((2, HEADS, DK, DV), BF16),
            vmem((4, DK, DV), BF16),
            vmem((GROUPS, 1, TILE), F32),
            vmem((GROUPS, TILE), F32),
            vmem((GROUPS, TILE), jnp.int32),
            vmem((24, TILE), F32),
            vmem((HEADS, 24, DV), F32),
            vmem(states, F32),
            vmem((ROWS, HEADS * DK), F32),
            vmem((ROWS, HEADS * DK), F32),
            vmem((ROWS, HEADS * DV), F32),
            vmem((ROWS, HEADS * DK), BF16),
            vmem((ROWS, HEADS * DK), BF16),
            vmem((ROWS, HEADS * DV), BF16),
            dma((7,)),
            dma((2 * PIECES + 2,)),
            dma((2 * PIECES + 2,)),
            dma((10,)),
            dma((10,)),
            dma((10,)),
            dma((10,)),
            dma((4,)),
            dma((4,)),
            dma((7,)),
            dma((7,)),
            dma((5,)),
        ],
        compiler_params=pltpu.CompilerParams(
            collective_id=0, has_side_effects=True, vmem_limit_bytes=56 * 2**20
        ),
        cost_estimate=pl.CostEstimate(
            flops=7_000_000_000, bytes_accessed=14_000_000, transcendentals=2_000_000
        ),
    )(query, keys, values, out_grad, out_weight, log_decay, block_order)
    return pl.pallas_call(
        hand_over,
        name="hand_over",
        out_shape=tuple(jax.ShapeDtypeStruct(g.shape, g.dtype) for g in grads),
        in_specs=[anywhere] * 3,
        out_specs=(anywhere,) * 3,
        scratch_shapes=[vmem(g.shape, g.dtype) for g in grads] + [dma((6,)), dma((6,))],
        compiler_params=pltpu.CompilerParams(vmem_limit_bytes=56 * 2**20),
        cost_estimate=pl.CostEstimate(flops=0, bytes_accessed=6_000_000, transcendentals=0),
    )(*grads)


def solution(mesh):
    placed = (
        P("ctx", "head"),
        P("ctx", "head"),
        P("ctx", "head"),
        P("ctx", "head"),
        P("head", None),
        P("head", "ctx"),
        P(),
    )
    return jax.shard_map(
        on_device,
        mesh=mesh,
        in_specs=placed,
        out_specs=(P("ctx", "head"), P("ctx", "head"), P("ctx", "head")),
        check_vma=False,
    )
```

```python
import jax
import jax.numpy as jnp
from jax import lax
from jax.experimental import pallas as pl
from jax.experimental.pallas import tpu as pltpu
from jax.sharding import PartitionSpec as P

MESH = pl.DeviceIdType.MESH
F32 = jnp.float32
BF16 = jnp.bfloat16
HEADS = 4
DK = 128
DV = 256
BLK = 384
ROWS = 768
COLS = 512
TILE = 128
GROUPS = 32
SCALE = DK ** -0.5

NT = (((1,), (1,)), ((), ()))
NN = (((1,), (0,)), ((), ()))
TN = (((0,), (0,)), ((), ()))


def dot(a, b, dims):
    return lax.dot_general(a, b, dims, preferred_element_type=F32)


def exact_dot(a, b, dims):
    return lax.dot_general(
        a, b, dims, preferred_element_type=F32, precision=lax.Precision.HIGHEST
    )


PIECES = 6
RELAYS = ((1, 1), (2, 3), (3, 4))
PASS_RELAYS = ((0, 3), (1, 4))
CHAINED = {1: (2, 2), -1: (2, 2)}


def kernel(
    q_hbm, k_hbm, v_hbm, og_hbm, w_hbm, ld_hbm, bo_hbm,
    dq_hbm, dk_hbm, dv_hbm,
    q, k, v, og, w, ld, bo,
    lrow, lcol, qdec, kdec, qpt, dec, probs,
    part, d_out, m_sum,
    n_own, n_one, n_two, n_via, m_own, m_one, m_two, m_via, relay,
    totals, total_rows, order_rows, factors, weights, a_sum,
    dq_sum, dk_sum, dv_sum, dq_out, dk_out, dv_out,
    loc_sem, og_ss, og_rs, n_ss, n_rs, m_ss, m_rs, relay_ss, relay_rs, t_ss, t_rs, out_sem,
):
    c = lax.axis_index("ctx")
    p = lax.axis_index("head")
    x = lax.rem(c, 4)
    y = lax.rem(c // 4, 4)
    zh = c // 16
    at16 = lax.rem(c, 16)
    core_mate = p + 1 - 2 * lax.rem(p, 2)
    z_mate = lax.rem(p + 2, 4)
    diag_mate = lax.rem(core_mate + 2, 4)
    later = lax.rem(c + 1, GROUPS)
    earlier = lax.rem(c + GROUPS - 1, GROUPS)
    x_peers = [c - x + lax.rem(x + a, 4) for a in (1, 2, 3)]
    y_peers = [c - 4 * y + 4 * lax.rem(y + a, 4) for a in (1, 2, 3)]
    zh_peer = lax.rem(c + 16, GROUPS)
    last = at16 == 15
    first = at16 == 0

    def beside(group, step):
        column = lax.rem(group, 4)
        return group - column + lax.rem(column + step, 4)

    right, left = beside(c, 1), beside(c, 3)
    n_target = lax.rem(right + 2, GROUPS)
    m_target = lax.rem(left + GROUPS - 2, GROUPS)
    n_helper = beside(lax.rem(c + GROUPS - 2, GROUPS), 3)
    m_helper = beside(lax.rem(c + 2, GROUPS), 1)

    local = [
        pltpu.make_async_copy(src, dst, loc_sem.at[i])
        for i, (src, dst) in enumerate(
            ((ld_hbm, ld), (bo_hbm, bo), (k_hbm, k), (v_hbm, v), (q_hbm, q),
             (og_hbm, og.at[0]), (w_hbm, w))
        )
    ]
    ld_in, bo_in, k_in, v_in, q_in, og_in, w_in = local

    barrier = pltpu.get_barrier_semaphore()

    def greet(to, who):
        pl.semaphore_signal(barrier, inc=1, device_id=(to, who), device_id_type=MESH)

    partners = [(c, core_mate), (c, z_mate), (zh_peer, p)]
    partners += [(peer, p) for peer in x_peers + y_peers]
    for to, who in partners:
        greet(to, who)
    others = (
        (later, x == 3), (earlier, x == 0),
        (n_target, (x == 1) | (x == 2)), (n_helper, x < 2),
        (m_target, (x == 1) | (x == 2)), (m_helper, x > 1),
    )
    for to, apart in others:
        pl.when(apart)(lambda to=to: greet(to, p))
    for _, step in RELAYS:
        pl.when(last)(lambda step=step: greet(later + step, p))
        pl.when(first)(lambda step=step: greet(earlier - step, p))
        pl.when(at16 == step)(lambda step=step: greet(lax.rem(c - step - 1 + GROUPS, GROUPS), p))
        pl.when(at16 == 15 - step)(lambda step=step: greet(lax.rem(c + step + 1, GROUPS), p))
    for copy in local:
        copy.start()
    relaying = sum(
        [((at16 == step) | (at16 == 15 - step)).astype(jnp.int32) for _, step in RELAYS]
    )
    next_only = ((at16 == 1) | (at16 == 14)).astype(jnp.int32)
    pl.semaphore_wait(
        barrier, len(partners) + sum(apart.astype(jnp.int32) for _, apart in others) + 3 * (last | first).astype(jnp.int32) + relaying
    )

    def send(src, dst, ss, rs, to):
        return pltpu.make_async_remote_copy(
            src_ref=src, dst_ref=dst, send_sem=ss, recv_sem=rs, device_id=to, device_id_type=MESH
        )

    def rows_of(b):
        return pl.ds(b * BLK, BLK)

    def piece_of(i):
        return pl.ds(i * TILE, TILE)

    z_copy = [
        send(og_hbm.at[piece_of(i)], og.at[2, piece_of(i)], og_ss.at[i], og_rs.at[i], (c, z_mate))
        for i in range(PIECES)
    ]
    diag_copy = [
        send(og.at[2, piece_of(i)], og.at[3, piece_of(i)], og_ss.at[PIECES + i],
             og_rs.at[PIECES + i], (c, core_mate))
        for i in range(PIECES)
    ]
    core_copy = [
        send(og_hbm.at[rows_of(b)], og.at[1, rows_of(b)], og_ss.at[2 * PIECES + b],
             og_rs.at[2 * PIECES + b], (c, core_mate))
        for b in (0, 1)
    ]
    n_flow = (n_own, n_one, n_two, n_via, n_ss, n_rs, later, left, n_target, 1)
    m_flow = (m_own, m_one, m_two, m_via, m_ss, m_rs, earlier, right, m_target, -1)

    def wraps(sign):
        return last if sign == 1 else first

    def half(h):
        return pl.ds(2 * h, 2)

    def first_hop(flow, b, h):
        own, one, _, _, ss, rs, to, _, _, _ = flow
        return send(own.at[b, half(h)], one.at[b, half(h)], ss.at[2 * b + h], rs.at[2 * b + h], (to, p))

    def chained(flow, b):
        return CHAINED[flow[-1]][b]

    def second_hop(flow, b):
        _, one, two, _, ss, rs, to, _, _, _ = flow
        heads = pl.ds(0, chained(flow, b))
        return send(one.at[b, heads], two.at[b, heads], ss.at[4 + b], rs.at[4 + b], (to, p))

    def both_arrive(flow, b):
        _, one, two, _, ss, rs, to, _, _, _ = flow
        return send(one.at[b], two.at[b], ss.at[4 + b], rs.at[4 + b], (to, p))

    def side_hop(flow, b):
        own, _, _, via, ss, rs, _, to, _, _ = flow
        k = chained(flow, b)
        return send(own.at[b, pl.ds(k, HEADS - k)], via.at[b, pl.ds(0, HEADS - k)],
                    ss.at[6 + b], rs.at[6 + b], (to, p))

    def side_second_hop(flow, b):
        _, _, two, via, ss, rs, _, _, to, _ = flow
        k = chained(flow, b)
        return send(via.at[b, pl.ds(0, HEADS - k)], two.at[b, pl.ds(k, HEADS - k)],
                    ss.at[8 + b], rs.at[4 + b], (to, p))

    def to_relays(flow, b, h):
        own, one, _, _, ss, rs, to, _, _, sign = flow
        for n in (2 * h, 2 * h + 1):
            if n == 0:
                send(own.at[b, n], one.at[b, n], ss.at[2 * b], rs.at[2 * b], (to, p)).start()
            else:
                send(own.at[b, n], relay.at[b], ss.at[2 * b + h], relay_rs.at[b],
                     (to + sign * RELAYS[n - 1][1], p)).start()

    def start(flow, b, h):
        @pl.when(jnp.logical_not(wraps(flow[-1])))
        def _():
            first_hop(flow, b, h).start()

        @pl.when(wraps(flow[-1]))
        def _():
            to_relays(flow, b, h)

        if h == 0 and chained(flow, b) < HEADS:
            side_hop(flow, b).start()

    def pass_chain(flow, b):
        _, one, two, _, ss, rs, to, _, _, sign = flow
        k = chained(flow, b)
        first_hop(flow, b, 0).wait_recv()
        if k > 2:
            first_hop(flow, b, 1).wait_recv()

        @pl.when(jnp.logical_not(wraps(sign)))
        def _():
            second_hop(flow, b).start()

        @pl.when(wraps(sign))
        def _():
            for n, step in PASS_RELAYS:
                send(one.at[b, n], relay.at[2 + b], ss.at[4 + b], relay_rs.at[2 + b],
                     (to + sign * step, p)).start()
            if k > 2:
                heads = pl.ds(2, k - 2)
                send(one.at[b, heads], two.at[b, heads], ss.at[4 + b], rs.at[4 + b],
                     (to, p)).start()

    def pass_side(flow, b):
        if chained(flow, b) < HEADS:
            side_hop(flow, b).wait_recv()
            side_second_hop(flow, b).start()

    def pass_relay(flow, slot):
        _, one, two, _, _, rs, _, _, _, sign = flow
        b = slot % 2
        for n, step in RELAYS if slot < 2 else PASS_RELAYS:
            @pl.when(at16 == (step if sign == 1 else 15 - step))
            def _(n=n, step=step):
                to = (c - sign * step, p)
                sem = 2 * b + n // 2 if slot < 2 else 4 + b
                send(relay.at[slot], relay.at[slot], relay_ss.at[slot], relay_rs.at[slot],
                     to).wait_recv()
                send(relay.at[slot], (one if slot < 2 else two).at[b, n], relay_ss.at[slot],
                     rs.at[sem], to).start()

    def sent(flow, b):
        first_hop(flow, b, 0).wait_send()
        first_hop(flow, b, 1).wait_send()
        second_hop(flow, b).wait_send()
        if chained(flow, b) < HEADS:
            side_hop(flow, b).wait_send()
            side_second_hop(flow, b).wait_send()

    tx_copy = [
        send(totals.at[pl.ds(c, 1)], totals.at[pl.ds(c, 1)], t_ss.at[a], t_rs.at[a], (x_peers[a], p))
        for a in range(3)
    ]
    ty_copy = [
        send(totals.at[pl.ds(c - x, 4)], totals.at[pl.ds(c - x, 4)], t_ss.at[3 + a], t_rs.at[3 + a],
             (y_peers[a], p))
        for a in range(3)
    ]
    tz_copy = send(
        totals.at[pl.ds(zh * 16, 16)], totals.at[pl.ds(zh * 16, 16)], t_ss.at[6], t_rs.at[6],
        (zh_peer, p),
    )

    for copy in core_copy + z_copy[:3]:
        copy.start()

    ld_in.wait()
    logs = jnp.concatenate([ld[:, :BLK], ld[:, BLK:]], axis=0)
    up_to = (
        lax.broadcasted_iota(jnp.int32, (BLK, BLK), 0)
        <= lax.broadcasted_iota(jnp.int32, (BLK, BLK), 1)
    ).astype(F32)
    lrow[...] = exact_dot(logs, up_to, NN).reshape(8, 1, BLK)
    total = exact_dot(logs, jnp.ones((BLK, TILE), F32), NN)
    mine = lax.broadcasted_iota(jnp.int32, (8, TILE), 1) // 16 == lax.broadcasted_iota(
        jnp.int32, (8, TILE), 0
    )
    totals[pl.ds(c, 1)] = jnp.sum(jnp.where(mine, total, 0.0), axis=0).reshape(1, 1, TILE)
    for copy in tx_copy:
        copy.start()
    columns = exact_dot(up_to, logs, (((0,), (1,)), ((), ())))
    for j in range(8):
        column = jnp.broadcast_to(columns[:, j : j + 1], (BLK, TILE))
        lcol[j] = column
        qdec[j] = jnp.exp(column)
        kdec[j] = jnp.exp(total[j : j + 1, :] - column)

    def key_cols(h):
        return pl.ds(pl.multiple_of(h * DK, DK), DK)

    def value_cols(h):
        return pl.ds(pl.multiple_of(h * DV, DV), DV)

    k_in.wait()
    v_in.wait()
    for b in (0, 1):
        for h in range(HEADS):
            scaled = (k[rows_of(b), key_cols(h)].astype(F32) * kdec[b * 4 + h]).astype(BF16)
            n_own[b, h] = dot(scaled, v[rows_of(b), value_cols(h)], TN).astype(BF16)
        start(n_flow, b, 0)
        start(n_flow, b, 1)

    q_in.wait()

    def early_part(b, h):
        j = b * 4 + h
        scaled = (q[rows_of(b), key_cols(h)].astype(F32) * qdec[j]).astype(BF16)
        qpt[j] = jnp.transpose(scaled)
        for i in range(3):
            at = i * TILE
            width = BLK - at
            gap = lrow[j][:, at:] - jnp.concatenate(
                [lcol[j, pl.ds(at, TILE)]] * (width // TILE), axis=1
            )
            on = lax.broadcasted_iota(jnp.int32, (TILE, width), 1) >= lax.broadcasted_iota(
                jnp.int32, (TILE, width), 0
            )
            decay = jnp.where(on, jnp.exp(jnp.minimum(gap, 0.0)), 0.0) * SCALE
            dec[j, pl.ds(at, TILE), pl.ds(at, width)] = decay
            scores = dot(
                k[pl.ds(b * BLK + at, TILE), key_cols(h)],
                q[pl.ds(b * BLK + at, width), key_cols(h)],
                NT,
            )
            probs[j, pl.ds(at, TILE), pl.ds(at, width)] = (scores * decay).astype(BF16)

    for j in range(8):
        early_part(j // 4, j % 4)
    for copy in z_copy[3:]:
        copy.start()

    def product(slot, owner, rows):
        return dot(
            og[slot, rows], w[:, pl.ds(pl.multiple_of(owner * COLS, COLS), COLS)], NT
        )

    og_in.wait()
    w_in.wait()
    for b in (0, 1):
        core_copy[b].wait_recv()
        part[rows_of(b)] = product(0, p, rows_of(b)) + product(1, core_mate, rows_of(b))

    def late_part(b, h):
        j = b * 4 + h
        for i in range(3):
            at = i * TILE
            width = BLK - at
            s_rows = pl.ds(b * BLK + at, TILE)
            t_rows = pl.ds(b * BLK + at, width)
            grads = d_out[t_rows, value_cols(h)]
            scores = dot(v[s_rows, value_cols(h)], grads, NT)
            grad_weights = (scores * dec[j, pl.ds(at, TILE), pl.ds(at, width)]).astype(BF16)
            dv_sum[s_rows, value_cols(h)] = dot(
                probs[j, pl.ds(at, TILE), pl.ds(at, width)], grads, NN
            )
            dk_sum[s_rows, key_cols(h)] = dot(grad_weights, q[t_rows, key_cols(h)], NN)
            to_query = dot(grad_weights, k[s_rows, key_cols(h)], TN)
            if i == 0:
                dq_sum[t_rows, key_cols(h)] = to_query
            else:
                dq_sum[t_rows, key_cols(h)] += to_query

    def forward(i):
        z_copy[i].wait_recv()
        diag_copy[i].start()

    def gather(first_piece, pieces):
        rows = pl.ds(first_piece * TILE, pieces * TILE)
        part[rows] += product(2, z_mate, rows)
        for i in range(first_piece, first_piece + pieces):
            diag_copy[i].wait_recv()
        d_out[rows] = (part[rows] + product(3, diag_mate, rows)).astype(BF16)

    n_aside = (at16 != 13) & (at16 != 14)

    forward(0)
    pl.when(n_aside)(lambda: pass_side(n_flow, 0))
    forward(1)
    pl.when(n_aside)(lambda: pass_side(n_flow, 1))
    forward(2)
    for copy in tx_copy:
        copy.wait_recv()
    for copy in ty_copy:
        copy.start()
    gather(0, 3)
    for h in range(HEADS):
        m_own[0, h] = dot(qpt[h], d_out[rows_of(0), value_cols(h)], NN).astype(BF16)
    start(m_flow, 0, 0)

    @pl.when(jnp.logical_not(first))
    def _():
        pass_chain(n_flow, 0)

    forward(3)
    for h in range(HEADS):
        late_part(0, h)
    start(m_flow, 0, 1)

    @pl.when(jnp.logical_not(first))
    def _():
        pass_chain(n_flow, 1)

    pass_relay(n_flow, 0)
    pass_relay(n_flow, 1)

    def weighted(n, state, h):
        return weights[h, n : n + 1] * state.astype(F32)

    forward(4)
    gather(3, 2)
    forward(5)
    for h in range(HEADS):
        m_sum[h] = dot(qpt[4 + h, :, :256], d_out[pl.ds(BLK, 256), value_cols(h)], NN)
    gather(5, 1)
    for h in range(HEADS):
        m_own[1, h] = (
            m_sum[h] + dot(qpt[4 + h, :, 256:], d_out[piece_of(5), value_cols(h)], NN)
        ).astype(BF16)
    start(m_flow, 1, 0)
    start(m_flow, 1, 1)
    for copy in ty_copy:
        copy.wait_recv()
    tz_copy.start()
    pass_side(m_flow, 0)
    pl.when(jnp.logical_not(last))(lambda: pass_chain(m_flow, 0))
    for h in range(HEADS):
        late_part(1, h)
    pass_relay(m_flow, 0)
    pass_side(m_flow, 1)
    pl.when(last)(lambda: pass_chain(m_flow, 0))
    pass_chain(m_flow, 1)
    pass_relay(m_flow, 1)

    @pl.when(jnp.logical_not(n_aside))
    def _():
        pass_side(n_flow, 0)
        pass_side(n_flow, 1)

    @pl.when(first)
    def _():
        pass_chain(n_flow, 0)
        pass_chain(n_flow, 1)

    pass_relay(n_flow, 2)
    pass_relay(n_flow, 3)
    pass_relay(m_flow, 2)
    tz_copy.wait_recv()
    bo_in.wait()

    def place(group, b):
        return bo[2 * group + b]

    own = [place(c, b) for b in (0, 1)]
    late = [place(lax.rem(c + d, GROUPS), b) for d in (1, 2) for b in (0, 1)]
    early = [place(lax.rem(c + GROUPS - d, GROUPS), b) for d in (1, 2) for b in (0, 1)]
    pairs = [(o, own[b]) for b in (0, 1) for o in [own[1 - b]] + late]
    pairs += [(own[b], o) for b in (0, 1) for o in early]
    first_half = lax.broadcasted_iota(jnp.int32, (1, TILE), 1) < 64
    for g in range(GROUPS):
        total_rows[g : g + 1] = totals[g]
        order_rows[g : g + 1] = jnp.where(first_half, bo[2 * g], bo[2 * g + 1])
    for n, (hi, lo) in enumerate(pairs):
        at = order_rows[...]
        gap = jnp.sum(
            jnp.where((at > lo) & (at < hi), total_rows[...], 0.0), axis=0, keepdims=True
        )
        gap = gap + jnp.concatenate([gap[:, 64:], gap[:, :64]], axis=1)
        seen = jnp.full((1, TILE), hi, jnp.int32) > lo
        factors[n : n + 1] = jnp.where(seen, jnp.exp(gap), 0.0) * SCALE
    for h in range(HEADS):
        weights[h] = jnp.broadcast_to(factors[:, h * 16 : h * 16 + 1], (24, DV))

    dq_done = pltpu.make_async_copy(dq_out, dq_hbm, out_sem.at[0])

    def finish_query():
        for b in (0, 1):
            if chained(n_flow, b) <= 2:
                first_hop(n_flow, b, 1).wait_recv()
            both_arrive(n_flow, b).wait_recv()
        for b in (0, 1):
            for h in range(HEADS):
                state = weighted(5 * (1 - b), n_own[1 - b, h], h)
                for i, source in enumerate((n_one, n_two)):
                    for other in (0, 1):
                        state = state + weighted(10 + 4 * b + 2 * i + other, source[other, h], h)
                rest = dot(d_out[rows_of(b), value_cols(h)], state.astype(BF16), NT)
                dq_out[rows_of(b), key_cols(h)] = (
                    dq_sum[rows_of(b), key_cols(h)] + rest * qdec[b * 4 + h]
                ).astype(BF16)
        dq_done.start()

    query_last = at16 <= 1
    pl.when(jnp.logical_not(query_last))(finish_query)

    pass_relay(m_flow, 3)
    for b in (0, 1):
        if chained(m_flow, b) <= 2:
            first_hop(m_flow, b, 1).wait_recv()
    both_arrive(m_flow, 0).wait_recv()
    for b in (0, 1):
        for h in range(HEADS):
            state = weighted(5 * b, m_own[1 - b, h], h)
            for n, source in ((1, m_one[0, h]), (2, m_one[1, h]), (3, m_two[0, h])):
                state = state + weighted(5 * b + n, source, h)
            a_sum[b, h] = state
    both_arrive(m_flow, 1).wait_recv()
    done = [dq_done]
    for b in (0, 1):
        for h in range(HEADS):
            state = (a_sum[b, h] + weighted(5 * b + 4, m_two[1, h], h)).astype(BF16)
            decay = kdec[b * 4 + h]
            to_value = dot(k[rows_of(b), key_cols(h)], state, NN)
            to_key = dot(v[rows_of(b), value_cols(h)], state, NT)
            dv_out[rows_of(b), value_cols(h)] = (
                dv_sum[rows_of(b), value_cols(h)]
                + to_value * jnp.concatenate([decay, decay], axis=1)
            ).astype(BF16)
            dk_out[rows_of(b), key_cols(h)] = (
                dk_sum[rows_of(b), key_cols(h)] + to_key * decay
            ).astype(BF16)
        done.append(
            pltpu.make_async_copy(dk_out.at[rows_of(b)], dk_hbm.at[rows_of(b)], out_sem.at[1 + b])
        )
        done.append(
            pltpu.make_async_copy(dv_out.at[rows_of(b)], dv_hbm.at[rows_of(b)], out_sem.at[3 + b])
        )
        done[-2].start()
        done[-1].start()
    pl.when(query_last)(finish_query)
    for copy in z_copy + core_copy + diag_copy:
        copy.wait_send()
    for b in (0, 1):
        sent(n_flow, b)
        sent(m_flow, b)

    for slot in range(4):
        @pl.when(relaying > (0 if slot < 2 else next_only))
        def _(slot=slot):
            send(relay.at[slot], relay.at[slot], relay_ss.at[slot], relay_rs.at[slot],
                 (later, p)).wait_send()

    for copy in tx_copy + ty_copy + [tz_copy]:
        copy.wait_send()
    for copy in done:
        copy.wait()


def hand_over(a, b, d, a_out, b_out, d_out, a_in, b_in, d_in, in_sems, out_sems):
    parts = [
        (array, held, out, pl.ds(n * 192, 192))
        for array, held, out in ((d, d_in, d_out), (a, a_in, a_out), (b, b_in, b_out))
        for n in range(4)
    ]
    ins = [
        pltpu.make_async_copy(array.at[rows], held.at[rows], in_sems.at[i])
        for i, (array, held, _, rows) in enumerate(parts)
    ]
    outs = [
        pltpu.make_async_copy(held.at[rows], out.at[rows], out_sems.at[i])
        for i, (_, held, out, rows) in enumerate(parts)
    ]
    for copy in ins:
        copy.start()
    for come, go in zip(ins, outs):
        come.wait()
        go.start()
    for copy in outs:
        copy.wait()


def on_device(query, keys, values, out_grad, out_weight, log_decay, block_order):
    anywhere = pl.BlockSpec(memory_space=pl.ANY)
    vmem = pltpu.VMEM
    states = (2, HEADS, DK, DV)
    dma = pltpu.SemaphoreType.DMA
    grads = pl.pallas_call(
        kernel,
        name="retention_backward",
        out_shape=(
            jax.ShapeDtypeStruct((ROWS, HEADS * DK), BF16),
            jax.ShapeDtypeStruct((ROWS, HEADS * DK), BF16),
            jax.ShapeDtypeStruct((ROWS, HEADS * DV), BF16),
        ),
        in_specs=[anywhere] * 7,
        out_specs=(anywhere,) * 3,
        scratch_shapes=[
            vmem((ROWS, HEADS * DK), BF16),
            vmem((ROWS, HEADS * DK), BF16),
            vmem((ROWS, HEADS * DV), BF16),
            vmem((4, ROWS, COLS), BF16),
            vmem((HEADS * DV, 4 * COLS), BF16),
            vmem((HEADS, ROWS), F32),
            pltpu.SMEM((2 * GROUPS,), jnp.int32),
            vmem((8, 1, BLK), F32),
            vmem((8, BLK, TILE), F32),
            vmem((8, BLK, TILE), F32),
            vmem((8, BLK, TILE), F32),
            vmem((8, DK, BLK), BF16),
            vmem((8, BLK, BLK), F32),
            vmem((8, BLK, BLK), BF16),
            vmem((ROWS, HEADS * DV), F32),
            vmem((ROWS, HEADS * DV), BF16),
            vmem((HEADS, DK, DV), F32),
            vmem(states, BF16),
            vmem(states, BF16),
            vmem(states, BF16),
            vmem((2, HEADS, DK, DV), BF16),
            vmem(states, BF16),
            vmem(states, BF16),
            vmem(states, BF16),
            vmem((2, HEADS, DK, DV), BF16),
            vmem((4, DK, DV), BF16),
            vmem((GROUPS, 1, TILE), F32),
            vmem((GROUPS, TILE), F32),
            vmem((GROUPS, TILE), jnp.int32),
            vmem((24, TILE), F32),
            vmem((HEADS, 24, DV), F32),
            vmem(states, F32),
            vmem((ROWS, HEADS * DK), F32),
            vmem((ROWS, HEADS * DK), F32),
            vmem((ROWS, HEADS * DV), F32),
            vmem((ROWS, HEADS * DK), BF16),
            vmem((ROWS, HEADS * DK), BF16),
            vmem((ROWS, HEADS * DV), BF16),
            dma((7,)),
            dma((2 * PIECES + 2,)),
            dma((2 * PIECES + 2,)),
            dma((10,)),
            dma((10,)),
            dma((10,)),
            dma((10,)),
            dma((4,)),
            dma((4,)),
            dma((7,)),
            dma((7,)),
            dma((5,)),
        ],
        compiler_params=pltpu.CompilerParams(
            collective_id=0, has_side_effects=True, vmem_limit_bytes=56 * 2**20
        ),
        cost_estimate=pl.CostEstimate(
            flops=7_000_000_000, bytes_accessed=14_000_000, transcendentals=2_000_000
        ),
    )(query, keys, values, out_grad, out_weight, log_decay, block_order)
    return pl.pallas_call(
        hand_over,
        name="hand_over",
        out_shape=tuple(jax.ShapeDtypeStruct(g.shape, g.dtype) for g in grads),
        in_specs=[anywhere] * 3,
        out_specs=(anywhere,) * 3,
        scratch_shapes=[vmem(g.shape, g.dtype) for g in grads] + [dma((12,)), dma((12,))],
        compiler_params=pltpu.CompilerParams(vmem_limit_bytes=56 * 2**20),
        cost_estimate=pl.CostEstimate(flops=0, bytes_accessed=6_000_000, transcendentals=0),
    )(*grads)


def solution(mesh):
    placed = (
        P("ctx", "head"),
        P("ctx", "head"),
        P("ctx", "head"),
        P("ctx", "head"),
        P("head", None),
        P("head", "ctx"),
        P(),
    )
    return jax.shard_map(
        on_device,
        mesh=mesh,
        in_specs=placed,
        out_specs=(P("ctx", "head"), P("ctx", "head"), P("ctx", "head")),
        check_vma=False,
    )
```

```python
import jax
import jax.numpy as jnp
from jax import lax
from jax.experimental import pallas as pl
from jax.experimental.pallas import tpu as pltpu
from jax.sharding import PartitionSpec as P

MESH = pl.DeviceIdType.MESH
F32 = jnp.float32
BF16 = jnp.bfloat16
HEADS = 4
DK = 128
DV = 256
BLK = 384
ROWS = 768
COLS = 512
TILE = 128
GROUPS = 32
SCALE = DK ** -0.5

NT = (((1,), (1,)), ((), ()))
NN = (((1,), (0,)), ((), ()))
TN = (((0,), (0,)), ((), ()))


def dot(a, b, dims):
    return lax.dot_general(a, b, dims, preferred_element_type=F32)


def exact_dot(a, b, dims):
    return lax.dot_general(
        a, b, dims, preferred_element_type=F32, precision=lax.Precision.HIGHEST
    )


PIECES = 6
RELAYS = ((1, 1), (2, 3), (3, 4))
PASS_RELAYS = ((0, 3), (1, 4))
CHAINED = {1: (2, 2), -1: (2, 2)}


def kernel(
    q_hbm, k_hbm, v_hbm, og_hbm, w_hbm, ld_hbm, bo_hbm,
    dq_hbm, dk_hbm, dv_hbm,
    q, k, v, og, w, ld, bo,
    lrow, lcol, qdec, kdec, qpt, dec, probs,
    part, d_out, m_sum,
    n_own, n_one, n_two, n_via, m_own, m_one, m_two, m_via, relay,
    totals, total_rows, order_rows, factors, weights, a_sum,
    dq_sum, dk_sum, dv_sum, dq_out, dk_out, dv_out,
    loc_sem, og_ss, og_rs, n_ss, n_rs, m_ss, m_rs, relay_ss, relay_rs, t_ss, t_rs, out_sem,
):
    c = lax.axis_index("ctx")
    p = lax.axis_index("head")
    x = lax.rem(c, 4)
    y = lax.rem(c // 4, 4)
    zh = c // 16
    at16 = lax.rem(c, 16)
    core_mate = p + 1 - 2 * lax.rem(p, 2)
    z_mate = lax.rem(p + 2, 4)
    diag_mate = lax.rem(core_mate + 2, 4)
    later = lax.rem(c + 1, GROUPS)
    earlier = lax.rem(c + GROUPS - 1, GROUPS)
    x_peers = [c - x + lax.rem(x + a, 4) for a in (1, 2, 3)]
    y_peers = [c - 4 * y + 4 * lax.rem(y + a, 4) for a in (1, 2, 3)]
    zh_peer = lax.rem(c + 16, GROUPS)
    last = at16 == 15
    first = at16 == 0

    def beside(group, step):
        column = lax.rem(group, 4)
        return group - column + lax.rem(column + step, 4)

    right, left = beside(c, 1), beside(c, 3)
    n_target = lax.rem(right + 2, GROUPS)
    m_target = lax.rem(left + GROUPS - 2, GROUPS)
    n_helper = beside(lax.rem(c + GROUPS - 2, GROUPS), 3)
    m_helper = beside(lax.rem(c + 2, GROUPS), 1)

    local = [
        pltpu.make_async_copy(src, dst, loc_sem.at[i])
        for i, (src, dst) in enumerate(
            ((ld_hbm, ld), (bo_hbm, bo), (k_hbm, k), (v_hbm, v), (q_hbm, q),
             (og_hbm, og.at[0]), (w_hbm, w))
        )
    ]
    ld_in, bo_in, k_in, v_in, q_in, og_in, w_in = local

    barrier = pltpu.get_barrier_semaphore()

    def greet(to, who):
        pl.semaphore_signal(barrier, inc=1, device_id=(to, who), device_id_type=MESH)

    partners = [(c, core_mate), (c, z_mate), (zh_peer, p)]
    partners += [(peer, p) for peer in x_peers + y_peers]
    for to, who in partners:
        greet(to, who)
    others = (
        (later, x == 3), (earlier, x == 0),
        (n_target, (x == 1) | (x == 2)), (n_helper, x < 2),
        (m_target, (x == 1) | (x == 2)), (m_helper, x > 1),
    )
    for to, apart in others:
        pl.when(apart)(lambda to=to: greet(to, p))
    for _, step in RELAYS:
        pl.when(last)(lambda step=step: greet(later + step, p))
        pl.when(first)(lambda step=step: greet(earlier - step, p))
        pl.when(at16 == step)(lambda step=step: greet(lax.rem(c - step - 1 + GROUPS, GROUPS), p))
        pl.when(at16 == 15 - step)(lambda step=step: greet(lax.rem(c + step + 1, GROUPS), p))
    for copy in local:
        copy.start()
    relaying = sum(
        [((at16 == step) | (at16 == 15 - step)).astype(jnp.int32) for _, step in RELAYS]
    )
    next_only = ((at16 == 1) | (at16 == 14)).astype(jnp.int32)
    pl.semaphore_wait(
        barrier, len(partners) + sum(apart.astype(jnp.int32) for _, apart in others) + 3 * (last | first).astype(jnp.int32) + relaying
    )

    def send(src, dst, ss, rs, to):
        return pltpu.make_async_remote_copy(
            src_ref=src, dst_ref=dst, send_sem=ss, recv_sem=rs, device_id=to, device_id_type=MESH
        )

    def rows_of(b):
        return pl.ds(b * BLK, BLK)

    def piece_of(i):
        return pl.ds(i * TILE, TILE)

    z_copy = [
        send(og_hbm.at[piece_of(i)], og.at[2, piece_of(i)], og_ss.at[i], og_rs.at[i], (c, z_mate))
        for i in range(PIECES)
    ]
    diag_copy = [
        send(og.at[2, piece_of(i)], og.at[3, piece_of(i)], og_ss.at[PIECES + i],
             og_rs.at[PIECES + i], (c, core_mate))
        for i in range(PIECES)
    ]
    core_copy = [
        send(og_hbm.at[rows_of(b)], og.at[1, rows_of(b)], og_ss.at[2 * PIECES + b],
             og_rs.at[2 * PIECES + b], (c, core_mate))
        for b in (0, 1)
    ]
    n_flow = (n_own, n_one, n_two, n_via, n_ss, n_rs, later, left, n_target, 1)
    m_flow = (m_own, m_one, m_two, m_via, m_ss, m_rs, earlier, right, m_target, -1)

    def wraps(sign):
        return last if sign == 1 else first

    def half(h):
        return pl.ds(2 * h, 2)

    def first_hop(flow, b, h):
        own, one, _, _, ss, rs, to, _, _, _ = flow
        return send(own.at[b, half(h)], one.at[b, half(h)], ss.at[2 * b + h], rs.at[2 * b + h], (to, p))

    def chained(flow, b):
        return CHAINED[flow[-1]][b]

    def second_hop(flow, b):
        _, one, two, _, ss, rs, to, _, _, _ = flow
        heads = pl.ds(0, chained(flow, b))
        return send(one.at[b, heads], two.at[b, heads], ss.at[4 + b], rs.at[4 + b], (to, p))

    def both_arrive(flow, b):
        _, one, two, _, ss, rs, to, _, _, _ = flow
        return send(one.at[b], two.at[b], ss.at[4 + b], rs.at[4 + b], (to, p))

    def side_hop(flow, b):
        own, _, _, via, ss, rs, _, to, _, _ = flow
        k = chained(flow, b)
        return send(own.at[b, pl.ds(k, HEADS - k)], via.at[b, pl.ds(0, HEADS - k)],
                    ss.at[6 + b], rs.at[6 + b], (to, p))

    def side_second_hop(flow, b):
        _, _, two, via, ss, rs, _, _, to, _ = flow
        k = chained(flow, b)
        return send(via.at[b, pl.ds(0, HEADS - k)], two.at[b, pl.ds(k, HEADS - k)],
                    ss.at[8 + b], rs.at[4 + b], (to, p))

    def to_relays(flow, b, h):
        own, one, _, _, ss, rs, to, _, _, sign = flow
        for n in (2 * h, 2 * h + 1):
            if n == 0:
                send(own.at[b, n], one.at[b, n], ss.at[2 * b], rs.at[2 * b], (to, p)).start()
            else:
                send(own.at[b, n], relay.at[b], ss.at[2 * b + h], relay_rs.at[b],
                     (to + sign * RELAYS[n - 1][1], p)).start()

    def start(flow, b, h):
        @pl.when(jnp.logical_not(wraps(flow[-1])))
        def _():
            first_hop(flow, b, h).start()

        @pl.when(wraps(flow[-1]))
        def _():
            to_relays(flow, b, h)

        if h == 0 and chained(flow, b) < HEADS:
            side_hop(flow, b).start()

    def pass_chain(flow, b):
        _, one, two, _, ss, rs, to, _, _, sign = flow
        k = chained(flow, b)
        first_hop(flow, b, 0).wait_recv()
        if k > 2:
            first_hop(flow, b, 1).wait_recv()

        @pl.when(jnp.logical_not(wraps(sign)))
        def _():
            second_hop(flow, b).start()

        @pl.when(wraps(sign))
        def _():
            for n, step in PASS_RELAYS:
                send(one.at[b, n], relay.at[2 + b], ss.at[4 + b], relay_rs.at[2 + b],
                     (to + sign * step, p)).start()
            if k > 2:
                heads = pl.ds(2, k - 2)
                send(one.at[b, heads], two.at[b, heads], ss.at[4 + b], rs.at[4 + b],
                     (to, p)).start()

    def pass_side(flow, b):
        if chained(flow, b) < HEADS:
            side_hop(flow, b).wait_recv()
            side_second_hop(flow, b).start()

    def pass_relay(flow, slot):
        _, one, two, _, _, rs, _, _, _, sign = flow
        b = slot % 2
        for n, step in RELAYS if slot < 2 else PASS_RELAYS:
            @pl.when(at16 == (step if sign == 1 else 15 - step))
            def _(n=n, step=step):
                to = (c - sign * step, p)
                sem = 2 * b + n // 2 if slot < 2 else 4 + b
                send(relay.at[slot], relay.at[slot], relay_ss.at[slot], relay_rs.at[slot],
                     to).wait_recv()
                send(relay.at[slot], (one if slot < 2 else two).at[b, n], relay_ss.at[slot],
                     rs.at[sem], to).start()

    def sent(flow, b):
        first_hop(flow, b, 0).wait_send()
        first_hop(flow, b, 1).wait_send()
        second_hop(flow, b).wait_send()
        if chained(flow, b) < HEADS:
            side_hop(flow, b).wait_send()
            side_second_hop(flow, b).wait_send()

    tx_copy = [
        send(totals.at[pl.ds(c, 1)], totals.at[pl.ds(c, 1)], t_ss.at[a], t_rs.at[a], (x_peers[a], p))
        for a in range(3)
    ]
    ty_copy = [
        send(totals.at[pl.ds(c - x, 4)], totals.at[pl.ds(c - x, 4)], t_ss.at[3 + a], t_rs.at[3 + a],
             (y_peers[a], p))
        for a in range(3)
    ]
    tz_copy = send(
        totals.at[pl.ds(zh * 16, 16)], totals.at[pl.ds(zh * 16, 16)], t_ss.at[6], t_rs.at[6],
        (zh_peer, p),
    )

    for copy in core_copy + z_copy[:3]:
        copy.start()

    ld_in.wait()
    logs = jnp.concatenate([ld[:, :BLK], ld[:, BLK:]], axis=0)
    up_to = (
        lax.broadcasted_iota(jnp.int32, (BLK, BLK), 0)
        <= lax.broadcasted_iota(jnp.int32, (BLK, BLK), 1)
    ).astype(F32)
    total = exact_dot(logs, jnp.ones((BLK, TILE), F32), NN)
    mine = lax.broadcasted_iota(jnp.int32, (8, TILE), 1) // 16 == lax.broadcasted_iota(
        jnp.int32, (8, TILE), 0
    )
    totals[pl.ds(c, 1)] = jnp.sum(jnp.where(mine, total, 0.0), axis=0).reshape(1, 1, TILE)
    for copy in tx_copy:
        copy.start()
    columns = exact_dot(up_to, logs, (((0,), (1,)), ((), ())))
    for j in range(8):
        column = jnp.broadcast_to(columns[:, j : j + 1], (BLK, TILE))
        lcol[j] = column
        kdec[j] = jnp.exp(total[j : j + 1, :] - column)

    def key_cols(h):
        return pl.ds(pl.multiple_of(h * DK, DK), DK)

    def value_cols(h):
        return pl.ds(pl.multiple_of(h * DV, DV), DV)

    k_in.wait()
    v_in.wait()
    for b in (0, 1):
        for h in range(HEADS):
            scaled = (k[rows_of(b), key_cols(h)].astype(F32) * kdec[b * 4 + h]).astype(BF16)
            n_own[b, h] = dot(scaled, v[rows_of(b), value_cols(h)], TN).astype(BF16)
        start(n_flow, b, 0)
        start(n_flow, b, 1)

    lrow[...] = exact_dot(logs, up_to, NN).reshape(8, 1, BLK)
    for j in range(8):
        qdec[j] = jnp.exp(lcol[j])
    q_in.wait()

    def early_part(b, h):
        j = b * 4 + h
        scaled = (q[rows_of(b), key_cols(h)].astype(F32) * qdec[j]).astype(BF16)
        qpt[j] = jnp.transpose(scaled)
        for i in range(3):
            at = i * TILE
            width = BLK - at
            gap = lrow[j][:, at:] - jnp.concatenate(
                [lcol[j, pl.ds(at, TILE)]] * (width // TILE), axis=1
            )
            on = lax.broadcasted_iota(jnp.int32, (TILE, width), 1) >= lax.broadcasted_iota(
                jnp.int32, (TILE, width), 0
            )
            decay = jnp.where(on, jnp.exp(jnp.minimum(gap, 0.0)), 0.0) * SCALE
            dec[j, pl.ds(at, TILE), pl.ds(at, width)] = decay
            scores = dot(
                k[pl.ds(b * BLK + at, TILE), key_cols(h)],
                q[pl.ds(b * BLK + at, width), key_cols(h)],
                NT,
            )
            probs[j, pl.ds(at, TILE), pl.ds(at, width)] = (scores * decay).astype(BF16)

    for j in range(8):
        early_part(j // 4, j % 4)
    for copy in z_copy[3:]:
        copy.start()

    def product(slot, owner, rows):
        return dot(
            og[slot, rows], w[:, pl.ds(pl.multiple_of(owner * COLS, COLS), COLS)], NT
        )

    og_in.wait()
    w_in.wait()
    for b in (0, 1):
        core_copy[b].wait_recv()
        part[rows_of(b)] = product(0, p, rows_of(b)) + product(1, core_mate, rows_of(b))

    def late_part(b, h):
        j = b * 4 + h
        for i in range(3):
            at = i * TILE
            width = BLK - at
            s_rows = pl.ds(b * BLK + at, TILE)
            t_rows = pl.ds(b * BLK + at, width)
            grads = d_out[t_rows, value_cols(h)]
            scores = dot(v[s_rows, value_cols(h)], grads, NT)
            grad_weights = (scores * dec[j, pl.ds(at, TILE), pl.ds(at, width)]).astype(BF16)
            dv_sum[s_rows, value_cols(h)] = dot(
                probs[j, pl.ds(at, TILE), pl.ds(at, width)], grads, NN
            )
            dk_sum[s_rows, key_cols(h)] = dot(grad_weights, q[t_rows, key_cols(h)], NN)
            to_query = dot(grad_weights, k[s_rows, key_cols(h)], TN)
            if i == 0:
                dq_sum[t_rows, key_cols(h)] = to_query
            else:
                dq_sum[t_rows, key_cols(h)] += to_query

    def forward(i):
        z_copy[i].wait_recv()
        diag_copy[i].start()

    def gather(first_piece, pieces):
        rows = pl.ds(first_piece * TILE, pieces * TILE)
        part[rows] += product(2, z_mate, rows)
        for i in range(first_piece, first_piece + pieces):
            diag_copy[i].wait_recv()
        d_out[rows] = (part[rows] + product(3, diag_mate, rows)).astype(BF16)

    n_aside = (at16 != 13) & (at16 != 14)

    forward(0)
    pl.when(n_aside)(lambda: pass_side(n_flow, 0))
    forward(1)
    pl.when(n_aside)(lambda: pass_side(n_flow, 1))
    forward(2)
    for copy in tx_copy:
        copy.wait_recv()
    for copy in ty_copy:
        copy.start()
    gather(0, 3)
    for h in range(HEADS):
        m_own[0, h] = dot(qpt[h], d_out[rows_of(0), value_cols(h)], NN).astype(BF16)
    start(m_flow, 0, 0)

    @pl.when(jnp.logical_not(first))
    def _():
        pass_chain(n_flow, 0)

    forward(3)
    for h in range(HEADS):
        late_part(0, h)
    start(m_flow, 0, 1)

    @pl.when(jnp.logical_not(first))
    def _():
        pass_chain(n_flow, 1)

    pass_relay(n_flow, 0)
    pass_relay(n_flow, 1)

    def weighted(n, state, h):
        return weights[h, n : n + 1] * state.astype(F32)

    forward(4)
    gather(3, 2)
    forward(5)
    for h in range(HEADS):
        m_sum[h] = dot(qpt[4 + h, :, :256], d_out[pl.ds(BLK, 256), value_cols(h)], NN)
    gather(5, 1)
    for h in range(HEADS):
        m_own[1, h] = (
            m_sum[h] + dot(qpt[4 + h, :, 256:], d_out[piece_of(5), value_cols(h)], NN)
        ).astype(BF16)
    start(m_flow, 1, 0)
    start(m_flow, 1, 1)
    for copy in ty_copy:
        copy.wait_recv()
    tz_copy.start()
    pass_side(m_flow, 0)
    pl.when(jnp.logical_not(last))(lambda: pass_chain(m_flow, 0))
    for h in range(HEADS):
        late_part(1, h)
    pass_relay(m_flow, 0)
    pass_side(m_flow, 1)
    pl.when(last)(lambda: pass_chain(m_flow, 0))
    pass_chain(m_flow, 1)
    pass_relay(m_flow, 1)

    @pl.when(jnp.logical_not(n_aside))
    def _():
        pass_side(n_flow, 0)
        pass_side(n_flow, 1)

    @pl.when(first)
    def _():
        pass_chain(n_flow, 0)
        pass_chain(n_flow, 1)

    pass_relay(n_flow, 2)
    pass_relay(n_flow, 3)
    pass_relay(m_flow, 2)
    tz_copy.wait_recv()
    bo_in.wait()

    def place(group, b):
        return bo[2 * group + b]

    own = [place(c, b) for b in (0, 1)]
    late = [place(lax.rem(c + d, GROUPS), b) for d in (1, 2) for b in (0, 1)]
    early = [place(lax.rem(c + GROUPS - d, GROUPS), b) for d in (1, 2) for b in (0, 1)]
    pairs = [(o, own[b]) for b in (0, 1) for o in [own[1 - b]] + late]
    pairs += [(own[b], o) for b in (0, 1) for o in early]
    first_half = lax.broadcasted_iota(jnp.int32, (1, TILE), 1) < 64
    for g in range(GROUPS):
        total_rows[g : g + 1] = totals[g]
        order_rows[g : g + 1] = jnp.where(first_half, bo[2 * g], bo[2 * g + 1])
    for n, (hi, lo) in enumerate(pairs):
        at = order_rows[...]
        gap = jnp.sum(
            jnp.where((at > lo) & (at < hi), total_rows[...], 0.0), axis=0, keepdims=True
        )
        gap = gap + jnp.concatenate([gap[:, 64:], gap[:, :64]], axis=1)
        seen = jnp.full((1, TILE), hi, jnp.int32) > lo
        factors[n : n + 1] = jnp.where(seen, jnp.exp(gap), 0.0) * SCALE
    for h in range(HEADS):
        weights[h] = jnp.broadcast_to(factors[:, h * 16 : h * 16 + 1], (24, DV))

    dq_done = pltpu.make_async_copy(dq_out, dq_hbm, out_sem.at[0])

    def finish_query():
        for b in (0, 1):
            if chained(n_flow, b) <= 2:
                first_hop(n_flow, b, 1).wait_recv()
            both_arrive(n_flow, b).wait_recv()
        for b in (0, 1):
            for h in range(HEADS):
                state = weighted(5 * (1 - b), n_own[1 - b, h], h)
                for i, source in enumerate((n_one, n_two)):
                    for other in (0, 1):
                        state = state + weighted(10 + 4 * b + 2 * i + other, source[other, h], h)
                rest = dot(d_out[rows_of(b), value_cols(h)], state.astype(BF16), NT)
                dq_out[rows_of(b), key_cols(h)] = (
                    dq_sum[rows_of(b), key_cols(h)] + rest * qdec[b * 4 + h]
                ).astype(BF16)
        dq_done.start()

    query_last = at16 <= 1
    pl.when(jnp.logical_not(query_last))(finish_query)

    pass_relay(m_flow, 3)
    for b in (0, 1):
        if chained(m_flow, b) <= 2:
            first_hop(m_flow, b, 1).wait_recv()
    both_arrive(m_flow, 0).wait_recv()
    for b in (0, 1):
        for h in range(HEADS):
            state = weighted(5 * b, m_own[1 - b, h], h)
            for n, source in ((1, m_one[0, h]), (2, m_one[1, h]), (3, m_two[0, h])):
                state = state + weighted(5 * b + n, source, h)
            a_sum[b, h] = state
    both_arrive(m_flow, 1).wait_recv()
    done = [dq_done]
    for b in (0, 1):
        for h in range(HEADS):
            state = (a_sum[b, h] + weighted(5 * b + 4, m_two[1, h], h)).astype(BF16)
            decay = kdec[b * 4 + h]
            to_value = dot(k[rows_of(b), key_cols(h)], state, NN)
            to_key = dot(v[rows_of(b), value_cols(h)], state, NT)
            dv_out[rows_of(b), value_cols(h)] = (
                dv_sum[rows_of(b), value_cols(h)]
                + to_value * jnp.concatenate([decay, decay], axis=1)
            ).astype(BF16)
            dk_out[rows_of(b), key_cols(h)] = (
                dk_sum[rows_of(b), key_cols(h)] + to_key * decay
            ).astype(BF16)
        done.append(
            pltpu.make_async_copy(dk_out.at[rows_of(b)], dk_hbm.at[rows_of(b)], out_sem.at[1 + b])
        )
        done.append(
            pltpu.make_async_copy(dv_out.at[rows_of(b)], dv_hbm.at[rows_of(b)], out_sem.at[3 + b])
        )
        done[-2].start()
        done[-1].start()
    pl.when(query_last)(finish_query)
    for copy in z_copy + core_copy + diag_copy:
        copy.wait_send()
    for b in (0, 1):
        sent(n_flow, b)
        sent(m_flow, b)

    for slot in range(4):
        @pl.when(relaying > (0 if slot < 2 else next_only))
        def _(slot=slot):
            send(relay.at[slot], relay.at[slot], relay_ss.at[slot], relay_rs.at[slot],
                 (later, p)).wait_send()

    for copy in tx_copy + ty_copy + [tz_copy]:
        copy.wait_send()
    for copy in done:
        copy.wait()


def hand_over(a, b, d, a_out, b_out, d_out, a_in, b_in, d_in, in_sems, out_sems):
    parts = [
        (array, held, out, pl.ds(n * 192, 192))
        for array, held, out in ((d, d_in, d_out), (a, a_in, a_out), (b, b_in, b_out))
        for n in range(4)
    ]
    ins = [
        pltpu.make_async_copy(array.at[rows], held.at[rows], in_sems.at[i])
        for i, (array, held, _, rows) in enumerate(parts)
    ]
    outs = [
        pltpu.make_async_copy(held.at[rows], out.at[rows], out_sems.at[i])
        for i, (_, held, out, rows) in enumerate(parts)
    ]
    for copy in ins:
        copy.start()
    for come, go in zip(ins, outs):
        come.wait()
        go.start()
    for copy in outs:
        copy.wait()


def on_device(query, keys, values, out_grad, out_weight, log_decay, block_order):
    anywhere = pl.BlockSpec(memory_space=pl.ANY)
    vmem = pltpu.VMEM
    states = (2, HEADS, DK, DV)
    dma = pltpu.SemaphoreType.DMA
    grads = pl.pallas_call(
        kernel,
        name="retention_backward",
        out_shape=(
            jax.ShapeDtypeStruct((ROWS, HEADS * DK), BF16),
            jax.ShapeDtypeStruct((ROWS, HEADS * DK), BF16),
            jax.ShapeDtypeStruct((ROWS, HEADS * DV), BF16),
        ),
        in_specs=[anywhere] * 7,
        out_specs=(anywhere,) * 3,
        scratch_shapes=[
            vmem((ROWS, HEADS * DK), BF16),
            vmem((ROWS, HEADS * DK), BF16),
            vmem((ROWS, HEADS * DV), BF16),
            vmem((4, ROWS, COLS), BF16),
            vmem((HEADS * DV, 4 * COLS), BF16),
            vmem((HEADS, ROWS), F32),
            pltpu.SMEM((2 * GROUPS,), jnp.int32),
            vmem((8, 1, BLK), F32),
            vmem((8, BLK, TILE), F32),
            vmem((8, BLK, TILE), F32),
            vmem((8, BLK, TILE), F32),
            vmem((8, DK, BLK), BF16),
            vmem((8, BLK, BLK), F32),
            vmem((8, BLK, BLK), BF16),
            vmem((ROWS, HEADS * DV), F32),
            vmem((ROWS, HEADS * DV), BF16),
            vmem((HEADS, DK, DV), F32),
            vmem(states, BF16),
            vmem(states, BF16),
            vmem(states, BF16),
            vmem((2, HEADS, DK, DV), BF16),
            vmem(states, BF16),
            vmem(states, BF16),
            vmem(states, BF16),
            vmem((2, HEADS, DK, DV), BF16),
            vmem((4, DK, DV), BF16),
            vmem((GROUPS, 1, TILE), F32),
            vmem((GROUPS, TILE), F32),
            vmem((GROUPS, TILE), jnp.int32),
            vmem((24, TILE), F32),
            vmem((HEADS, 24, DV), F32),
            vmem(states, F32),
            vmem((ROWS, HEADS * DK), F32),
            vmem((ROWS, HEADS * DK), F32),
            vmem((ROWS, HEADS * DV), F32),
            vmem((ROWS, HEADS * DK), BF16),
            vmem((ROWS, HEADS * DK), BF16),
            vmem((ROWS, HEADS * DV), BF16),
            dma((7,)),
            dma((2 * PIECES + 2,)),
            dma((2 * PIECES + 2,)),
            dma((10,)),
            dma((10,)),
            dma((10,)),
            dma((10,)),
            dma((4,)),
            dma((4,)),
            dma((7,)),
            dma((7,)),
            dma((5,)),
        ],
        compiler_params=pltpu.CompilerParams(
            collective_id=0, has_side_effects=True, vmem_limit_bytes=56 * 2**20
        ),
        cost_estimate=pl.CostEstimate(
            flops=7_000_000_000, bytes_accessed=14_000_000, transcendentals=2_000_000
        ),
    )(query, keys, values, out_grad, out_weight, log_decay, block_order)
    return pl.pallas_call(
        hand_over,
        name="hand_over",
        out_shape=tuple(jax.ShapeDtypeStruct(g.shape, g.dtype) for g in grads),
        in_specs=[anywhere] * 3,
        out_specs=(anywhere,) * 3,
        scratch_shapes=[vmem(g.shape, g.dtype) for g in grads] + [dma((12,)), dma((12,))],
        compiler_params=pltpu.CompilerParams(vmem_limit_bytes=56 * 2**20),
        cost_estimate=pl.CostEstimate(flops=0, bytes_accessed=6_000_000, transcendentals=0),
    )(*grads)


def solution(mesh):
    placed = (
        P("ctx", "head"),
        P("ctx", "head"),
        P("ctx", "head"),
        P("ctx", "head"),
        P("head", None),
        P("head", "ctx"),
        P(),
    )
    return jax.shard_map(
        on_device,
        mesh=mesh,
        in_specs=placed,
        out_specs=(P("ctx", "head"), P("ctx", "head"), P("ctx", "head")),
        check_vma=False,
    )
```
